128 devices in a mesh: lat: 8 (over y, core), lon: 8 (over x, z_lo), rep: 2 (over z_hi).
Axes of the slice: x: 4, y: 4, z: 4 (z_hi: 2, z_lo: 2; z = z_hi * 2 + z_lo), core: 2. Of those that a mesh axis runs over, the one named last changes fastest.
Arguments:
- fine_field: bfloat16 [4, 64, 256, 512], P('rep', 'lat', 'lon'), parts along dimension 0, may hold values from -6 to 6
- cotangent: bfloat16 [4, 64, 256, 512], P('rep', 'lat', 'lon'), parts along dimension 0, may hold values from -6 to 6
- land_sea: int32 [64, 256], replicated, may hold values 0 or 1
- shifts: int32 [2], replicated, may hold values from 1 to 7, as said below
- gain_attn: float32 [512], replicated, may hold values from 0.5 to 1.5
- w_qkv: bfloat16 [512, 1536], replicated, may hold values from -0.25 to 0.25
- w_proj: bfloat16 [512, 512], replicated, may hold values from -0.25 to 0.25
- land_bias: float32 [16], replicated, may hold values from -2 to 2
- gain_merge: float32 [2048], replicated, may hold values from 0.5 to 1.5
- w_merge: bfloat16 [2048, 1024], replicated, may hold values from -0.125 to 0.125
- w_expand: bfloat16 [1024, 2048], replicated, may hold values from -0.1875 to 0.1875
Outputs:
- output: bfloat16 [4, 64, 256, 512], P('rep', 'lat', 'lon'), parts along dimension 0
- grad_field: bfloat16 [4, 64, 256, 512], P('rep', 'lat', 'lon'), parts along dimension 0
- grad_qkv: float32 [1024, 1536], P(('rep', 'lat', 'lon')), parts along dimension 0
- grad_proj: float32 [1024, 512], P(('rep', 'lat', 'lon')), parts along dimension 0
- grad_merge: float32 [4096, 1024], P(('rep', 'lat', 'lon')), parts along dimension 0
- grad_expand: float32 [2048, 2048], P(('rep', 'lat', 'lon')), parts along dimension 0
The draws below stay inside these ranges and needn't reach their ends.
There are 2 independent parts, one for each index of `rep`. The reference program is written for one: setup_inputs(seed, part) draws one part's arguments, and reference() takes and returns one part's arrays. A program takes and returns all parts, laid end to end along the dimension named above; an argument that names none is the same for every part. Nothing has to cross between parts.
Inputs may be any that keep to these rules, and one draw needn't show every extreme that they name: `shifts`: one of the two entries is 7, the other lies from 1 to 6.
All inputs are finite; a program needn't handle non-finite values.
Results may differ from the reference program's by a relative error of at most 0.019.
Values may be sent and summed in bfloat16 or wider, within the bound.
A program may use at most 128 MiB of HBM per device.

```python
from functools import partial
import jax
import jax.numpy as jnp
from jax import lax

C = 512
HEADS = 16
WIN = 8
LV = 2
H = 64
W = 256


def draw_shifts(key, part):
    key = jax.random.fold_in(key, 7)
    first_key, second_key = jax.random.split(key)
    random_shift = jax.random.randint(first_key, (1,), 1, WIN - 1).astype(jnp.int32)
    chooser = jax.random.randint(second_key, (1,), 0, 2).astype(jnp.int32)
    largest = jnp.full((1,), WIN - 1, jnp.int32)
    return jnp.where(chooser == 0, jnp.concatenate((largest, random_shift)), jnp.concatenate((random_shift, largest))).astype(jnp.int32)


def plant(result, key, least, high):
    spot = [jax.random.randint(jax.random.fold_in(key, axis), (), 0, length) for axis, length in enumerate(result.shape)]
    main_axis = result.shape.index(max(result.shape))
    neighbour = spot[:main_axis] + [(spot[main_axis] + 1) % result.shape[main_axis]] + spot[main_axis + 1:]
    return result.at[tuple(spot)].set(least).at[tuple(neighbour)].set(high)


def shard_levels(rng, dims, pieces, smallest, top_value):
    factor_of, own = 1.0, jax.random.fold_in(rng, 6)
    for position, shards_of in pieces:
        draws = jnp.exp(jax.random.uniform(jax.random.fold_in(own, position), (shards_of,), jnp.float32, smallest / len(pieces), top_value / len(pieces)))
        factor_of = factor_of * jnp.repeat(draws, dims[position] // shards_of).reshape([-1 if axis == position else 1 for axis in range(len(dims))])
    return factor_of


def noise(rng, dims, spread, limit, pieces=(), held_as=jnp.bfloat16):
    result = spread * jax.random.normal(rng, dims, jnp.float32)
    if pieces:
        result = result * shard_levels(rng, dims, pieces, -0.22, 0.18)
    return jnp.clip(result, -limit, limit).astype(held_as)


def setup_inputs(seed: int = 0, part: int = 0) -> dict:
    splits = jax.random.split(jax.random.key(seed), 12)
    part_splits = jax.random.split(jax.random.fold_in(splits[11], part), 12)
    return {
        "fine_field": noise(part_splits[0], (LV, H, W, C), 1.0, 6.0, ((1, 8), (2, 8))),
        "cotangent": noise(part_splits[1], (LV, H, W, C), 1.0, 6.0, ((1, 8), (2, 8))),
        "land_sea": plant((jax.random.randint(splits[2], (H, W), 0, 10) < 3).astype(jnp.int32), jax.random.fold_in(splits[2], 1), 0, 1),
        "shifts": draw_shifts(jax.random.fold_in(splits[11], 71), part),
        "gain_attn": jnp.clip(1.0 + 0.1 * jax.random.normal(splits[4], (C,), jnp.float32), 0.5, 1.5),
        "w_qkv": noise(splits[5], (C, 3 * C), C ** -0.5, 0.25),
        "w_proj": noise(splits[6], (C, C), C ** -0.5, 0.25),
        "land_bias": jnp.clip(jax.random.uniform(splits[7], (HEADS,), jnp.float32, -2.0, 2.0), -2.0, 2.0),
        "gain_merge": jnp.clip(1.0 + 0.1 * jax.random.normal(splits[8], (4 * C,), jnp.float32), 0.5, 1.5),
        "w_merge": noise(splits[9], (4 * C, 2 * C), (4 * C) ** -0.5, 0.125),
        "w_expand": noise(splits[10], (2 * C, 4 * C), (2 * C) ** -0.5, 0.1875),
    }


epsilon = 1e-05

def layer_norm(values, scales):
    average = lax.optimization_barrier(jnp.mean(values, axis=-1, keepdims=True))
    centred = values - average
    variance = lax.optimization_barrier(jnp.mean(centred * centred, axis=-1, keepdims=True))
    return centred * lax.rsqrt(variance + epsilon) * scales

def to_windows(array, window):
    levels, row_count, col_count, features = array.shape
    shaped = array.reshape(levels, row_count // window, window, col_count // window, window, features)
    return shaped.transpose(1, 3, 0, 2, 4, 5).reshape(-1, levels * window * window, features)

def from_windows(array, levels, row_count, col_count, window):
    features = array.shape[-1]
    shaped = array.reshape(row_count // window, col_count // window, levels, window, window, features)
    return shaped.transpose(2, 0, 3, 1, 4, 5).reshape(levels, row_count, col_count, features)

def region_of(row_ids, total_rows, shift_lat):
    return (row_ids >= total_rows - WIN).astype(jnp.int32) + (row_ids >= total_rows - shift_lat).astype(jnp.int32)

def window_core(queries, window_keys, window_values, land_keys, region, land_bias):
    head_dim = queries.shape[-1]
    scores = jnp.einsum('wqhd,wkhd->whqk', queries.astype(jnp.float32), window_keys.astype(jnp.float32)) * head_dim ** (-0.5)
    scores = scores + land_bias[None, :, None, None] * land_keys[:, None, None, :]
    same_region = region[:, :, None] == region[:, None, :]
    scores = jnp.where(same_region[:, None, :, :], scores, -1000000000.0)
    weights = jax.nn.softmax(scores, axis=-1).astype(jnp.bfloat16)
    mixed_out = jnp.einsum('whqk,wkhd->wqhd', weights.astype(jnp.float32), window_values.astype(jnp.float32))
    return mixed_out.astype(jnp.bfloat16)

def attention_forward(rolled, land_rows, region_rows, gain_attn, w_qkv, w_proj, land_bias):
    levels, row_count, col_count, channels = rolled.shape
    head_count = land_bias.shape[0]
    normed = layer_norm(rolled.astype(jnp.float32), gain_attn).astype(jnp.bfloat16)
    projected = jnp.dot(normed.reshape(-1, channels), w_qkv, preferred_element_type=jnp.float32).astype(jnp.bfloat16)
    windows = to_windows(projected.reshape(levels, row_count, col_count, 3 * channels), WIN)
    windows = windows.reshape(windows.shape[0], windows.shape[1], 3, head_count, channels // head_count)
    land_grid = jnp.broadcast_to(land_rows.astype(jnp.float32)[None, :, :, None], (levels, row_count, col_count, 1))
    land_keys = to_windows(land_grid, WIN)[:, :, 0]
    region_grid = jnp.broadcast_to(region_rows[None, :, None, None], (levels, row_count, col_count, 1))
    region = to_windows(region_grid, WIN)[:, :, 0]
    mixed_out = window_core(windows[:, :, 0], windows[:, :, 1], windows[:, :, 2], land_keys, region, land_bias)
    attended = from_windows(mixed_out.reshape(mixed_out.shape[0], mixed_out.shape[1], channels), levels, row_count, col_count, WIN)
    branch = jnp.dot(attended.reshape(-1, channels), w_proj, preferred_element_type=jnp.float32).astype(jnp.bfloat16)
    saved = (rolled, normed, windows, land_keys, region, attended)
    return (branch.reshape(levels, row_count, col_count, channels), saved)

def attention_backward(saved, grad_branch, gain_attn, w_qkv, w_proj, land_bias):
    rolled, normed, windows, land_keys, region, attended = saved
    levels, row_count, col_count, channels = rolled.shape
    grad_flat = grad_branch.reshape(-1, channels)
    grad_proj = jnp.dot(attended.reshape(-1, channels).T, grad_flat, preferred_element_type=jnp.float32)
    grad_attended = jnp.dot(grad_flat, w_proj.T, preferred_element_type=jnp.float32).astype(jnp.bfloat16)
    grad_mixed = to_windows(grad_attended.reshape(levels, row_count, col_count, channels), WIN)
    grad_mixed = grad_mixed.reshape(windows.shape[0], windows.shape[1], windows.shape[3], windows.shape[4])

    def attend_only(queries, window_keys, window_values):
        return window_core(queries, window_keys, window_values, land_keys, region, land_bias)
    _unused, core_pullback = jax.vjp(attend_only, windows[:, :, 0], windows[:, :, 1], windows[:, :, 2])
    grad_q, grad_k, grad_v = core_pullback(grad_mixed)
    grad_windows = jnp.stack((grad_q, grad_k, grad_v), axis=2).reshape(windows.shape[0], windows.shape[1], 3 * channels)
    grad_projected = from_windows(grad_windows, levels, row_count, col_count, WIN).reshape(-1, 3 * channels)
    grad_qkv = jnp.dot(normed.reshape(-1, channels).T, grad_projected, preferred_element_type=jnp.float32)
    grad_normed = jnp.dot(grad_projected, w_qkv.T, preferred_element_type=jnp.float32)
    _unused, norm_pullback = jax.vjp(partial(layer_norm, scales=gain_attn), rolled.astype(jnp.float32).reshape(-1, channels))
    grad_rolled = norm_pullback(grad_normed)[0].astype(jnp.bfloat16).reshape(levels, row_count, col_count, channels)
    return (grad_rolled, grad_qkv, grad_proj)

def arrange(grid):
    levels, row_count, col_count, channels = grid.shape
    shaped = grid.reshape(levels, row_count // 2, 2, col_count // 2, 2, channels)
    return shaped.transpose(0, 1, 3, 2, 4, 5).reshape(-1, 4 * channels)

def unarrange(flat, levels, row_count, col_count):
    channels = flat.shape[-1] // 4
    shaped = flat.reshape(levels, row_count // 2, col_count // 2, 2, 2, channels)
    return shaped.transpose(0, 1, 3, 2, 4, 5).reshape(levels, row_count, col_count, channels)

def merge_pass(hidden, cotangent, gain_merge, w_merge, w_expand):
    levels, row_count, col_count, channels = hidden.shape
    merged_f = arrange(hidden).astype(jnp.float32)
    normed = layer_norm(merged_f, gain_merge).astype(jnp.bfloat16)
    coarse = jnp.dot(normed, w_merge, preferred_element_type=jnp.float32)
    activated, gelu_pullback = jax.vjp(jax.nn.gelu, coarse)
    activated = activated.astype(jnp.bfloat16)
    expanded = jnp.dot(activated, w_expand, preferred_element_type=jnp.float32)
    output = (hidden.astype(jnp.float32) + unarrange(expanded, levels, row_count, col_count)).astype(jnp.bfloat16)
    grad_up = arrange(cotangent)
    grad_expand = jnp.dot(activated.T, grad_up, preferred_element_type=jnp.float32)
    grad_activated = jnp.dot(grad_up, w_expand.T, preferred_element_type=jnp.float32)
    grad_coarse = gelu_pullback(grad_activated)[0].astype(jnp.bfloat16)
    grad_merge = jnp.dot(normed.T, grad_coarse, preferred_element_type=jnp.float32)
    grad_normed = jnp.dot(grad_coarse, w_merge.T, preferred_element_type=jnp.float32)
    _unused, norm_pullback = jax.vjp(partial(layer_norm, scales=gain_merge), merged_f)
    grad_hidden = cotangent.astype(jnp.float32) + unarrange(norm_pullback(grad_normed)[0], levels, row_count, col_count)
    return (output, grad_hidden, grad_merge, grad_expand)

def split_rows(grid, blocks):
    levels = grid.shape[0]
    return grid.reshape((levels, blocks, WIN) + grid.shape[2:]).swapaxes(0, 1)

def join_rows(grid):
    blocks = grid.shape[0]
    joined = grid.swapaxes(0, 1)
    return joined.reshape((joined.shape[0], blocks * WIN) + joined.shape[3:])

def reference(fine_field, cotangent, land_sea, shifts, gain_attn, w_qkv, w_proj, land_bias, gain_merge, w_merge, w_expand):
    levels, total_rows, total_cols, channels = fine_field.shape
    blocks = total_rows // WIN
    shift_lat = shifts[0]
    shift_lon = shifts[1]
    rolled = jnp.roll(fine_field, (-shift_lat, -shift_lon), axis=(1, 2))
    land_rolled = jnp.roll(land_sea, (-shift_lat, -shift_lon), axis=(0, 1))
    regions = region_of(jnp.arange(total_rows, dtype=jnp.int32), total_rows, shift_lat)
    rolled_blocks = split_rows(rolled, blocks)
    land_blocks = land_rolled.reshape(blocks, WIN, total_cols)
    region_blocks = regions.reshape(blocks, WIN)

    def forward_block(block_items):
        branch, _unused = attention_forward(block_items[0], block_items[1], block_items[2], gain_attn, w_qkv, w_proj, land_bias)
        return branch
    branch = join_rows(lax.map(forward_block, (rolled_blocks, land_blocks, region_blocks)))
    rolled_back = jnp.roll(branch, (shift_lat, shift_lon), axis=(1, 2))
    hidden = (fine_field.astype(jnp.float32) + rolled_back.astype(jnp.float32)).astype(jnp.bfloat16)

    def merge_step(totals, block_items):
        output, grad_hidden, grad_merge, grad_expand = merge_pass(block_items[0], block_items[1], gain_merge, w_merge, w_expand)
        return ((totals[0] + grad_merge, totals[1] + grad_expand), (output, grad_hidden))
    start_merge = (jnp.zeros(w_merge.shape, jnp.float32), jnp.zeros(w_expand.shape, jnp.float32))
    merge_totals, merge_outs = lax.scan(merge_step, start_merge, (split_rows(hidden, blocks), split_rows(cotangent, blocks)))
    output = join_rows(merge_outs[0])
    grad_hidden = join_rows(merge_outs[1])
    grad_branch = jnp.roll(grad_hidden.astype(jnp.bfloat16), (-shift_lat, -shift_lon), axis=(1, 2))

    def backward_step(totals, block_items):
        branch, saved = attention_forward(block_items[0], block_items[1], block_items[2], gain_attn, w_qkv, w_proj, land_bias)
        grad_rolled, grad_qkv, grad_proj = attention_backward(saved, block_items[3], gain_attn, w_qkv, w_proj, land_bias)
        return ((totals[0] + grad_qkv, totals[1] + grad_proj), grad_rolled)
    start_attn = (jnp.zeros(w_qkv.shape, jnp.float32), jnp.zeros(w_proj.shape, jnp.float32))
    attn_totals, grad_blocks = lax.scan(backward_step, start_attn, (rolled_blocks, land_blocks, region_blocks, split_rows(grad_branch, blocks)))
    grad_rolled = join_rows(grad_blocks)
    grad_back = jnp.roll(grad_rolled, (shift_lat, shift_lon), axis=(1, 2))
    grad_field = (grad_hidden + grad_back.astype(jnp.float32)).astype(jnp.bfloat16)
    return (output, grad_field, attn_totals[0], attn_totals[1], merge_totals[0], merge_totals[1])
```

```python
from functools import partial

import jax
import jax.numpy as jnp
from jax import lax
from jax.experimental import pallas as pl
from jax.experimental.pallas import tpu as pltpu
from jax.sharding import PartitionSpec as P

WIN = 8


epsilon = 1e-05


def from_behind(value, axis, steps):
    count = lax.axis_size(axis)
    pairs = [(source, (source + steps) % count) for source in range(count)]
    return lax.ppermute(value, axis, pairs)


def layer_norm(values, scales):
    average = jnp.mean(values, axis=-1, keepdims=True)
    centred = values - average
    variance = jnp.mean(centred * centred, axis=-1, keepdims=True)
    return centred * lax.rsqrt(variance + epsilon) * scales


def to_windows(array, window):
    levels, row_count, col_count, features = array.shape
    shaped = array.reshape(
        levels, row_count // window, window, col_count // window, window, features
    )
    return shaped.transpose(1, 3, 0, 2, 4, 5).reshape(-1, levels * window * window, features)


def from_windows(array, levels, row_count, col_count, window):
    features = array.shape[-1]
    shaped = array.reshape(
        row_count // window, col_count // window, levels, window, window, features
    )
    return shaped.transpose(2, 0, 3, 1, 4, 5).reshape(levels, row_count, col_count, features)


def region_of(row_ids, total_rows, shift_lat):
    return (row_ids >= total_rows - WIN).astype(jnp.int32) + (
        row_ids >= total_rows - shift_lat
    ).astype(jnp.int32)


def window_core(queries, window_keys, window_values, land_keys, region, land_bias):
    head_dim = queries.shape[-1]
    scores = jnp.einsum(
        "wqhd,wkhd->whqk", queries.astype(jnp.float32), window_keys.astype(jnp.float32)
    ) * head_dim ** (-0.5)
    scores = scores + land_bias[None, :, None, None] * land_keys[:, None, None, :]
    same_region = region[:, :, None] == region[:, None, :]
    scores = jnp.where(same_region[:, None, :, :], scores, -1000000000.0)
    weights = jax.nn.softmax(scores, axis=-1).astype(jnp.bfloat16)
    mixed_out = jnp.einsum(
        "whqk,wkhd->wqhd", weights.astype(jnp.float32), window_values.astype(jnp.float32)
    )
    return mixed_out.astype(jnp.bfloat16)


def attention_forward(rolled, land_rows, region_rows, gain_attn, w_qkv, w_proj, land_bias):
    levels, row_count, col_count, channels = rolled.shape
    head_count = land_bias.shape[0]
    normed = layer_norm(rolled.astype(jnp.float32), gain_attn).astype(jnp.bfloat16)
    projected = jnp.dot(
        normed.reshape(-1, channels), w_qkv, preferred_element_type=jnp.float32
    ).astype(jnp.bfloat16)
    windows = to_windows(projected.reshape(levels, row_count, col_count, 3 * channels), WIN)
    windows = windows.reshape(
        windows.shape[0], windows.shape[1], 3, head_count, channels // head_count
    )
    land_grid = jnp.broadcast_to(
        land_rows.astype(jnp.float32)[None, :, :, None], (levels, row_count, col_count, 1)
    )
    land_keys = to_windows(land_grid, WIN)[:, :, 0]
    region_grid = jnp.broadcast_to(
        region_rows[None, :, None, None], (levels, row_count, col_count, 1)
    )
    region = to_windows(region_grid, WIN)[:, :, 0]
    mixed_out = window_core(
        windows[:, :, 0], windows[:, :, 1], windows[:, :, 2], land_keys, region, land_bias
    )
    attended = from_windows(
        mixed_out.reshape(mixed_out.shape[0], mixed_out.shape[1], channels),
        levels,
        row_count,
        col_count,
        WIN,
    )
    branch = jnp.dot(
        attended.reshape(-1, channels), w_proj, preferred_element_type=jnp.float32
    ).astype(jnp.bfloat16)
    saved = (rolled, normed, windows, land_keys, region, attended)
    return (branch.reshape(levels, row_count, col_count, channels), saved)


def attention_backward(saved, grad_branch, gain_attn, w_qkv, w_proj, land_bias):
    rolled, normed, windows, land_keys, region, attended = saved
    levels, row_count, col_count, channels = rolled.shape
    grad_flat = grad_branch.reshape(-1, channels)
    grad_proj = jnp.dot(
        attended.reshape(-1, channels).T, grad_flat, preferred_element_type=jnp.float32
    )
    grad_attended = jnp.dot(grad_flat, w_proj.T, preferred_element_type=jnp.float32).astype(
        jnp.bfloat16
    )
    grad_mixed = to_windows(grad_attended.reshape(levels, row_count, col_count, channels), WIN)
    grad_mixed = grad_mixed.reshape(
        windows.shape[0], windows.shape[1], windows.shape[3], windows.shape[4]
    )

    def attend_only(queries, window_keys, window_values):
        return window_core(queries, window_keys, window_values, land_keys, region, land_bias)

    _unused, core_pullback = jax.vjp(
        attend_only, windows[:, :, 0], windows[:, :, 1], windows[:, :, 2]
    )
    grad_q, grad_k, grad_v = core_pullback(grad_mixed)
    grad_windows = jnp.stack((grad_q, grad_k, grad_v), axis=2).reshape(
        windows.shape[0], windows.shape[1], 3 * channels
    )
    grad_projected = from_windows(grad_windows, levels, row_count, col_count, WIN).reshape(
        -1, 3 * channels
    )
    grad_qkv = jnp.dot(
        normed.reshape(-1, channels).T, grad_projected, preferred_element_type=jnp.float32
    )
    grad_normed = jnp.dot(grad_projected, w_qkv.T, preferred_element_type=jnp.float32)
    _unused, norm_pullback = jax.vjp(
        partial(layer_norm, scales=gain_attn), rolled.astype(jnp.float32).reshape(-1, channels)
    )
    grad_rolled = (
        norm_pullback(grad_normed)[0]
        .astype(jnp.bfloat16)
        .reshape(levels, row_count, col_count, channels)
    )
    return (grad_rolled, grad_qkv, grad_proj)


def arrange(grid):
    levels, row_count, col_count, channels = grid.shape
    shaped = grid.reshape(levels, row_count // 2, 2, col_count // 2, 2, channels)
    return shaped.transpose(0, 1, 3, 2, 4, 5).reshape(-1, 4 * channels)


def unarrange(flat, levels, row_count, col_count):
    channels = flat.shape[-1] // 4
    shaped = flat.reshape(levels, row_count // 2, col_count // 2, 2, 2, channels)
    return shaped.transpose(0, 1, 3, 2, 4, 5).reshape(levels, row_count, col_count, channels)


def merge_pass(hidden, cotangent, gain_merge, w_merge, w_expand):
    levels, row_count, col_count, channels = hidden.shape
    merged_f = arrange(hidden).astype(jnp.float32)
    normed = layer_norm(merged_f, gain_merge).astype(jnp.bfloat16)
    coarse = jnp.dot(normed, w_merge, preferred_element_type=jnp.float32)
    activated, gelu_pullback = jax.vjp(jax.nn.gelu, coarse)
    activated = activated.astype(jnp.bfloat16)
    expanded = jnp.dot(activated, w_expand, preferred_element_type=jnp.float32)
    output = (
        hidden.astype(jnp.float32) + unarrange(expanded, levels, row_count, col_count)
    ).astype(jnp.bfloat16)
    grad_up = arrange(cotangent)
    grad_expand = jnp.dot(activated.T, grad_up, preferred_element_type=jnp.float32)
    grad_activated = jnp.dot(grad_up, w_expand.T, preferred_element_type=jnp.float32)
    grad_coarse = gelu_pullback(grad_activated)[0].astype(jnp.bfloat16)
    grad_merge = jnp.dot(normed.T, grad_coarse, preferred_element_type=jnp.float32)
    grad_normed = jnp.dot(grad_coarse, w_merge.T, preferred_element_type=jnp.float32)
    _unused, norm_pullback = jax.vjp(partial(layer_norm, scales=gain_merge), merged_f)
    grad_hidden = cotangent.astype(jnp.float32) + unarrange(
        norm_pullback(grad_normed)[0], levels, row_count, col_count
    )
    return (output, grad_hidden, grad_merge, grad_expand)


def roll_minus(grid, shift_lat, shift_lon):
    rim_width = WIN - 1
    rim_rows = lax.slice_in_dim(grid, 0, rim_width, axis=1)
    arrived = from_behind(rim_rows, "lat", -1)
    joined = jnp.concatenate((grid, arrived), axis=1)
    grid = lax.dynamic_slice_in_dim(joined, shift_lat, grid.shape[1], axis=1)
    rim_cols = lax.slice_in_dim(grid, 0, rim_width, axis=2)
    arrived = from_behind(rim_cols, "lon", -1)
    joined = jnp.concatenate((grid, arrived), axis=2)
    return lax.dynamic_slice_in_dim(joined, shift_lon, grid.shape[2], axis=2)


def roll_plus(grid, shift_lat, shift_lon):
    rim_width = WIN - 1
    row_total = grid.shape[1]
    rim_rows = lax.slice_in_dim(grid, row_total - rim_width, row_total, axis=1)
    arrived = from_behind(rim_rows, "lat", 1)
    joined = jnp.concatenate((arrived, grid), axis=1)
    grid = lax.dynamic_slice_in_dim(joined, rim_width - shift_lat, row_total, axis=1)
    col_total = grid.shape[2]
    rim_cols = lax.slice_in_dim(grid, col_total - rim_width, col_total, axis=2)
    arrived = from_behind(rim_cols, "lon", 1)
    joined = jnp.concatenate((arrived, grid), axis=2)
    return lax.dynamic_slice_in_dim(joined, rim_width - shift_lon, col_total, axis=2)


MESH = pl.DeviceIdType.MESH


class Ring:
    def __init__(self, place, right, left, block, store, bufs, send_sems, recv_sems, lead, half):
        self.place, self.right, self.left = place, right, left
        self.block, self.store = block, store
        self.bufs, self.outs = bufs[0], bufs[1]
        self.send_sems, self.recv_sems = send_sems, recv_sems
        self.lead, self.half = lead, half
        self.copies = {}

    def part(self, k, which):
        return self.block(k).at[:, :, pl.ds(which * self.half, self.half)]

    def copy(self, slot, source, target):
        made = pltpu.make_async_remote_copy(
            src_ref=source,
            dst_ref=self.bufs.at[slot],
            send_sem=self.send_sems.at[slot],
            recv_sem=self.recv_sems.at[slot],
            device_id=target,
            device_id_type=MESH,
        )
        made.start()
        self.copies[slot] = made

    def begin(self):
        ahead = lax.rem(self.place + 1, 4)
        across = lax.rem(self.place + 2, 4)
        behind = lax.rem(self.place + 3, 4)
        self.copy(0, self.part(across, 0), self.right)
        self.copy(3, self.part(across, 1), self.left)
        self.copy(1, self.part(ahead, 1), self.right)
        self.copy(4, self.part(behind, 0), self.left)

    def middle(self):
        ahead = lax.rem(self.place + 1, 4)
        behind = lax.rem(self.place + 3, 4)
        for slot, which, k, out, target in ((0, 0, ahead, 0, self.right), (3, 1, behind, 1, self.left)):
            self.copies[slot].wait_recv()

            def add(i, carry, slot=slot, which=which, k=k, out=out):
                mine = self.block(k)[i, :, pl.ds(which * self.half, self.half)]
                total = mine.astype(jnp.float32) + self.bufs[slot, i].astype(jnp.float32)
                self.outs[out, i] = total.astype(jnp.bfloat16)
                return carry

            lax.fori_loop(0, self.lead, add, 0)
            self.copy(2 if out == 0 else 5, self.outs.at[out], target)

    def finish(self):
        for slot in (1, 2, 4, 5):
            self.copies[slot].wait_recv()

        def add(i, carry):
            for which, first, second in ((0, 2, 4), (1, 5, 1)):
                mine = self.block(self.place)[i, :, pl.ds(which * self.half, self.half)]
                total = (
                    mine.astype(jnp.float32)
                    + self.bufs[first, i].astype(jnp.float32)
                    + self.bufs[second, i].astype(jnp.float32)
                )
                self.store(i, which, total)
            return carry

        lax.fori_loop(0, self.lead, add, 0)

    def drain(self):
        for slot in range(6):
            self.copies[slot].wait_send()


class Stream:
    def __init__(self, where, source, first_axis, scratch, store):
        red, buf1, out1, buf2, out2, fin, zsend, zrecv, ssem, rsem = scratch
        self.where, self.scratch, self.store = where, scratch, store
        self.rows, self.width = source.shape[2], source.shape[3]
        half = self.width // 2
        axes = {
            "y": (where["y"], where["up"], where["down"], lambda k: source.at[k]),
            "x": (where["x"], where["east"], where["west"], lambda k: source.at[:, k]),
        }
        second_axis = "x" if first_axis == "y" else "y"

        def store_red(i, which, total):
            red[i, 0, :, pl.ds(which * half, half)] = total.astype(jnp.bfloat16)

        def store_fin(i, which, total):
            deep = self.rows // 2
            for z in range(2):
                fin[z, :, pl.ds(which * half, half)] = total[z * deep : (z + 1) * deep]

        place, right, left, block = axes[first_axis]
        self.ring1 = Ring(
            place, right, left, block, store_red, (buf1, out1), ssem.at[pl.ds(0, 6)], rsem.at[pl.ds(0, 6)], 4, half
        )
        place, right, left, _unused = axes[second_axis]
        self.ring2 = Ring(
            place,
            right,
            left,
            lambda k: red.at[k],
            store_fin,
            (buf2, out2),
            ssem.at[pl.ds(6, 6)],
            rsem.at[pl.ds(6, 6)],
            1,
            half,
        )

    def z_begin(self):
        _r, _a, _b, _c, _d, fin, zsend, zrecv, ssem, rsem = self.scratch
        zsend[...] = fin[1 - self.where["z"]].astype(zsend.dtype)
        self.z_copy = pltpu.make_async_remote_copy(
            src_ref=zsend,
            dst_ref=zrecv,
            send_sem=ssem.at[12],
            recv_sem=rsem.at[12],
            device_id=self.where["beside"],
            device_id_type=MESH,
        )
        self.z_copy.start()

    def z_finish(self):
        fin, zrecv = self.scratch[5], self.scratch[7]
        self.z_copy.wait_recv()
        self.store(fin[self.where["z"]] + zrecv[...].astype(jnp.float32))

    def drain(self):
        self.ring1.drain()
        self.ring2.drain()
        self.z_copy.wait_send()


def stream_scratch(rows, width, z_type):
    half = width // 2
    deep = rows // 2
    return [
        pltpu.VMEM((4, 1, rows, width), jnp.bfloat16),
        pltpu.VMEM((6, 4, rows, half), jnp.bfloat16),
        pltpu.VMEM((2, 4, rows, half), jnp.bfloat16),
        pltpu.VMEM((6, 1, rows, half), jnp.bfloat16),
        pltpu.VMEM((2, 1, rows, half), jnp.bfloat16),
        pltpu.VMEM((2, deep, width), jnp.float32),
        pltpu.VMEM((deep, width), z_type),
        pltpu.VMEM((deep, width), z_type),
        pltpu.SemaphoreType.DMA((13,)),
        pltpu.SemaphoreType.DMA((13,)),
    ]


def places():
    lat, lon = lax.axis_index("lat"), lax.axis_index("lon")
    core, z = lax.rem(lat, 2), lax.rem(lon, 2)
    return {
        "lat": lat,
        "lon": lon,
        "y": lat // 2,
        "x": lon // 2,
        "core": core,
        "z": z,
        "up": {"lat": lax.rem(lat + 2, 8)},
        "down": {"lat": lax.rem(lat + 6, 8)},
        "east": {"lon": lax.rem(lon + 2, 8)},
        "west": {"lon": lax.rem(lon + 6, 8)},
        "beside": {"lon": lon + 1 - 2 * z},
        "sibling": {"lat": lat + 1 - 2 * core},
    }


def reduce_kernel(at_ref, ex_ref, mg_ref, qkv_out, proj_out, mg_out, ex_out, *scratch):
    where = places()
    core = where["core"]
    acc_at1, acc_at2, acc_ex, acc_mg, got_at, got_ex, got_mg, csem, crsem = scratch[:9]
    barrier = pltpu.get_barrier_semaphore()
    for name in ("up", "down", "east", "west", "beside", "sibling"):
        pl.semaphore_signal(barrier, inc=1, device_id=where[name], device_id_type=MESH)
    pl.semaphore_wait(barrier, 6)

    firsts = []
    for n, (source, target) in enumerate(((ex_ref, got_ex), (mg_ref, got_mg), (at_ref, got_at))):
        made = pltpu.make_async_remote_copy(
            src_ref=source.at[:, 1 - core],
            dst_ref=target,
            send_sem=csem.at[n],
            recv_sem=crsem.at[n],
            device_id=where["sibling"],
            device_id_type=MESH,
        )
        made.start()
        firsts.append(made)

    def store_at1(value):
        qkv_out[:, 0:1024] = value

    def store_at2(value):
        qkv_out[:, 1024:1536] = value[:, :512]
        proj_out[...] = value[:, 512:]

    def store_ex(value):
        ex_out[...] = value

    def store_mg(value):
        mg_out[...] = value

    streams = [
        Stream(where, acc_ex, "y", scratch[9:19], store_ex),
        Stream(where, acc_mg, "x", scratch[19:29], store_mg),
        Stream(where, acc_at1, "y", scratch[29:39], store_at1),
        Stream(where, acc_at2, "x", scratch[39:49], store_at2),
    ]

    def sum_into(source, got, targets):
        def add(n, carry):
            y, x = n // 4, lax.rem(n, 4)
            total = source[y, core, x].astype(jnp.float32) + got[y, x].astype(jnp.float32)
            total = total.astype(jnp.bfloat16)
            start = 0
            for target in targets:
                width = target.shape[3]
                target[y, x] = total[:, start : start + width]
                start += width
            return carry

        lax.fori_loop(0, 16, add, 0)

    firsts[0].wait_recv()
    sum_into(ex_ref, got_ex, [acc_ex])
    streams[0].ring1.begin()
    firsts[1].wait_recv()
    sum_into(mg_ref, got_mg, [acc_mg])
    streams[1].ring1.begin()
    firsts[2].wait_recv()
    sum_into(at_ref, got_at, [acc_at1, acc_at2])
    streams[2].ring1.begin()
    streams[3].ring1.begin()
    for stream in streams:
        stream.ring1.middle()
    for stream in streams:
        stream.ring1.finish()
        stream.ring2.begin()
    for stream in streams:
        stream.ring2.middle()
    for stream in streams:
        stream.ring2.finish()
        stream.z_begin()
    for stream in streams:
        stream.z_finish()
    for made in firsts:
        made.wait_send()
    for stream in streams:
        stream.drain()


def reduce_all(grad_qkv, grad_proj, grad_merge, grad_expand):
    at = jnp.concatenate((grad_qkv, grad_proj), axis=1).astype(jnp.bfloat16).reshape(4, 2, 4, 16, 2048)
    ex = grad_expand.astype(jnp.bfloat16).reshape(4, 2, 4, 32, 2048)
    mg = grad_merge.astype(jnp.bfloat16).reshape(4, 2, 4, 64, 1024)
    vmem = pl.BlockSpec(memory_space=pltpu.VMEM)
    bf16 = jnp.bfloat16
    return pl.pallas_call(
        reduce_kernel,
        out_shape=(
            jax.ShapeDtypeStruct((8, 1536), jnp.float32),
            jax.ShapeDtypeStruct((8, 512), jnp.float32),
            jax.ShapeDtypeStruct((32, 1024), jnp.float32),
            jax.ShapeDtypeStruct((16, 2048), jnp.float32),
        ),
        in_specs=[vmem] * 3,
        out_specs=(vmem,) * 4,
        scratch_shapes=[
            pltpu.VMEM((4, 4, 16, 1024), bf16),
            pltpu.VMEM((4, 4, 16, 1024), bf16),
            pltpu.VMEM((4, 4, 32, 2048), bf16),
            pltpu.VMEM((4, 4, 64, 1024), bf16),
            pltpu.VMEM((4, 4, 16, 2048), bf16),
            pltpu.VMEM((4, 4, 32, 2048), bf16),
            pltpu.VMEM((4, 4, 64, 1024), bf16),
            pltpu.SemaphoreType.DMA((3,)),
            pltpu.SemaphoreType.DMA((3,)),
        ]
        + stream_scratch(32, 2048, bf16)
        + stream_scratch(64, 1024, bf16)
        + stream_scratch(16, 1024, jnp.float32)
        + stream_scratch(16, 1024, jnp.float32),
        compiler_params=pltpu.CompilerParams(
            collective_id=0, has_side_effects=True, vmem_limit_bytes=56 * 2**20
        ),
        name="reduce_gradients",
    )(at, ex, mg)


def on_device(
    fine_field,
    cotangent,
    land_sea,
    shifts,
    gain_attn,
    w_qkv,
    w_proj,
    land_bias,
    gain_merge,
    w_merge,
    w_expand,
):
    levels, row_count, col_count, channels = fine_field.shape
    shift_lat = shifts[0]
    shift_lon = shifts[1]
    lat_index = lax.axis_index("lat")
    lon_index = lax.axis_index("lon")
    land_all = jnp.roll(land_sea, (-shift_lat, -shift_lon), axis=(0, 1))
    land_rolled = lax.dynamic_slice(
        land_all, (lat_index * row_count, lon_index * col_count), (row_count, col_count)
    )
    row_ids = lat_index * row_count + jnp.arange(row_count, dtype=jnp.int32)
    region_rows = region_of(row_ids, land_sea.shape[0], shift_lat)
    rolled = roll_minus(fine_field, shift_lat, shift_lon)
    branch, saved = attention_forward(
        rolled, land_rolled, region_rows, gain_attn, w_qkv, w_proj, land_bias
    )
    rolled_back = roll_plus(branch, shift_lat, shift_lon)
    hidden = (fine_field.astype(jnp.float32) + rolled_back.astype(jnp.float32)).astype(jnp.bfloat16)
    output, grad_hidden, grad_merge, grad_expand = merge_pass(
        hidden, cotangent, gain_merge, w_merge, w_expand
    )
    grad_branch = roll_minus(grad_hidden.astype(jnp.bfloat16), shift_lat, shift_lon)
    grad_rolled, grad_qkv, grad_proj = attention_backward(
        saved, grad_branch, gain_attn, w_qkv, w_proj, land_bias
    )
    grad_back = roll_plus(grad_rolled, shift_lat, shift_lon)
    grad_field = (grad_hidden + grad_back.astype(jnp.float32)).astype(jnp.bfloat16)
    reduced = reduce_all(grad_qkv, grad_proj, grad_merge, grad_expand)
    return (output, grad_field, reduced[0], reduced[1], reduced[2], reduced[3])


def solution(mesh):
    return jax.shard_map(
        on_device,
        mesh=mesh,
        in_specs=(
            P("rep", "lat", "lon", None),
            P("rep", "lat", "lon", None),
            P(),
            P(),
            P(),
            P(),
            P(),
            P(),
            P(),
            P(),
            P(),
        ),
        out_specs=(
            P("rep", "lat", "lon", None),
            P("rep", "lat", "lon", None),
            P(("rep", "lat", "lon"), None),
            P(("rep", "lat", "lon"), None),
            P(("rep", "lat", "lon"), None),
            P(("rep", "lat", "lon"), None),
        ),
        check_vma=False,
    )
```

```python
import jax
import jax.numpy as jnp
from jax import lax
from jax.experimental import pallas as pl
from jax.experimental.pallas import tpu as pltpu
from jax.sharding import PartitionSpec as P

epsilon = 1e-05

MESH = pl.DeviceIdType.MESH


class Ring:
    def __init__(self, place, right, left, block, store, bufs, send_sems, recv_sems, lead, half):
        self.place, self.right, self.left = place, right, left
        self.block, self.store = block, store
        self.bufs, self.outs = bufs[0], bufs[1]
        self.send_sems, self.recv_sems = send_sems, recv_sems
        self.lead, self.half = lead, half
        self.copies = {}

    def part(self, k, which):
        return self.block(k).at[:, :, pl.ds(which * self.half, self.half)]

    def copy(self, slot, source, target):
        made = pltpu.make_async_remote_copy(
            src_ref=source,
            dst_ref=self.bufs.at[slot],
            send_sem=self.send_sems.at[slot],
            recv_sem=self.recv_sems.at[slot],
            device_id=target,
            device_id_type=MESH,
        )
        made.start()
        self.copies[slot] = made

    def begin(self):
        ahead = lax.rem(self.place + 1, 4)
        across = lax.rem(self.place + 2, 4)
        behind = lax.rem(self.place + 3, 4)
        self.copy(0, self.part(across, 0), self.right)
        self.copy(3, self.part(across, 1), self.left)
        self.copy(1, self.part(ahead, 1), self.right)
        self.copy(4, self.part(behind, 0), self.left)

    def middle(self):
        ahead = lax.rem(self.place + 1, 4)
        behind = lax.rem(self.place + 3, 4)
        for slot, which, k, out, target in ((0, 0, ahead, 0, self.right), (3, 1, behind, 1, self.left)):
            self.copies[slot].wait_recv()

            def add(i, carry, slot=slot, which=which, k=k, out=out):
                mine = self.block(k)[i, :, pl.ds(which * self.half, self.half)]
                total = mine.astype(jnp.float32) + self.bufs[slot, i].astype(jnp.float32)
                self.outs[out, i] = total.astype(jnp.bfloat16)
                return carry

            lax.fori_loop(0, self.lead, add, 0)
            self.copy(2 if out == 0 else 5, self.outs.at[out], target)

    def finish(self):
        for slot in (1, 2, 4, 5):
            self.copies[slot].wait_recv()

        def add(i, carry):
            for which, first, second in ((0, 2, 4), (1, 5, 1)):
                mine = self.block(self.place)[i, :, pl.ds(which * self.half, self.half)]
                total = (
                    mine.astype(jnp.float32)
                    + self.bufs[first, i].astype(jnp.float32)
                    + self.bufs[second, i].astype(jnp.float32)
                )
                self.store(i, which, total)
            return carry

        lax.fori_loop(0, self.lead, add, 0)

    def drain(self):
        for slot in range(6):
            self.copies[slot].wait_send()


class Stream:
    def __init__(self, where, source, first_axis, scratch, store):
        red, buf1, out1, buf2, out2, fin, zsend, zrecv, ssem, rsem = scratch
        self.where, self.scratch, self.store = where, scratch, store
        self.rows, self.width = source.shape[2], source.shape[3]
        half = self.width // 2
        axes = {
            "y": (where["y"], where["up"], where["down"], lambda k: source.at[k]),
            "x": (where["x"], where["east"], where["west"], lambda k: source.at[:, k]),
        }
        second_axis = "x" if first_axis == "y" else "y"

        def store_red(i, which, total):
            red[i, 0, :, pl.ds(which * half, half)] = total.astype(jnp.bfloat16)

        def store_fin(i, which, total):
            deep = self.rows // 2
            for z in range(2):
                fin[z, :, pl.ds(which * half, half)] = total[z * deep : (z + 1) * deep]

        place, right, left, block = axes[first_axis]
        self.ring1 = Ring(
            place, right, left, block, store_red, (buf1, out1), ssem.at[pl.ds(0, 6)], rsem.at[pl.ds(0, 6)], 4, half
        )
        place, right, left, _unused = axes[second_axis]
        self.ring2 = Ring(
            place,
            right,
            left,
            lambda k: red.at[k],
            store_fin,
            (buf2, out2),
            ssem.at[pl.ds(6, 6)],
            rsem.at[pl.ds(6, 6)],
            1,
            half,
        )

    def z_begin(self):
        _r, _a, _b, _c, _d, fin, zsend, zrecv, ssem, rsem = self.scratch
        zsend[...] = fin[1 - self.where["z"]].astype(zsend.dtype)
        self.z_copy = pltpu.make_async_remote_copy(
            src_ref=zsend,
            dst_ref=zrecv,
            send_sem=ssem.at[12],
            recv_sem=rsem.at[12],
            device_id=self.where["beside"],
            device_id_type=MESH,
        )
        self.z_copy.start()

    def z_finish(self):
        fin, zrecv = self.scratch[5], self.scratch[7]
        self.z_copy.wait_recv()
        self.store(fin[self.where["z"]] + zrecv[...].astype(jnp.float32))

    def drain(self):
        self.ring1.drain()
        self.ring2.drain()
        self.z_copy.wait_send()


def stream_scratch(rows, width, z_type):
    half = width // 2
    deep = rows // 2
    return [
        pltpu.VMEM((4, 1, rows, width), jnp.bfloat16),
        pltpu.VMEM((6, 4, rows, half), jnp.bfloat16),
        pltpu.VMEM((2, 4, rows, half), jnp.bfloat16),
        pltpu.VMEM((6, 1, rows, half), jnp.bfloat16),
        pltpu.VMEM((2, 1, rows, half), jnp.bfloat16),
        pltpu.VMEM((2, deep, width), jnp.float32),
        pltpu.VMEM((deep, width), z_type),
        pltpu.VMEM((deep, width), z_type),
        pltpu.SemaphoreType.DMA((13,)),
        pltpu.SemaphoreType.DMA((13,)),
    ]


def places():
    lat, lon = lax.axis_index("lat"), lax.axis_index("lon")
    core, z = lax.rem(lat, 2), lax.rem(lon, 2)
    return {
        "lat": lat,
        "lon": lon,
        "y": lat // 2,
        "x": lon // 2,
        "core": core,
        "z": z,
        "up": {"lat": lax.rem(lat + 2, 8)},
        "down": {"lat": lax.rem(lat + 6, 8)},
        "east": {"lon": lax.rem(lon + 2, 8)},
        "west": {"lon": lax.rem(lon + 6, 8)},
        "beside": {"lon": lon + 1 - 2 * z},
        "sibling": {"lat": lat + 1 - 2 * core},
    }


def dot(a, b):
    return lax.dot_general(a, b, (((1,), (0,)), ((), ())), preferred_element_type=jnp.float32)


def dot_nt(a, b):
    return lax.dot_general(a, b, (((1,), (1,)), ((), ())), preferred_element_type=jnp.float32)


def dot_tn(a, b):
    return lax.dot_general(a, b, (((0,), (0,)), ((), ())), preferred_element_type=jnp.float32)


def code_of(row, col):
    return (row + 16) * 64 + (col + 16)


def fine_code(s):
    return code_of(s >> 5, s & 31)


def patch_code(s):
    quarter, coarse = s >> 6, s & 63
    return code_of(2 * (coarse >> 4) + (quarter >> 1), 2 * (coarse & 15) + (quarter & 1))


def window_code(s):
    return code_of((s & 63) >> 3, 8 * (s >> 6) + (s & 7))


def rim_code(t):
    kind, c4 = t >> 5, t & 3
    row = jnp.where(kind < 2, (t & 31) >> 2, ((t & 15) >> 2) + jnp.where(kind == 2, 8, -4))
    west = jnp.where(kind < 2, kind & 1, (t >> 4) & 1)
    return code_of(row, c4 + 32 - 36 * west)


def iota(shape, axis):
    return lax.broadcasted_iota(jnp.int32, shape, axis)


def one_hot(same):
    return jnp.where(same, 1.0, 0.0).astype(jnp.bfloat16)


def fill_gather(ref, target_code, source_code, offset):
    target = target_code(iota((256, 128), 0)) + offset
    lane = iota((1, 128), 1)
    half = (lane >> 5 << 6) + (lane & 31)
    pieces = (
        source_code(lane),
        source_code(lane + 128),
        source_code(half + 32) - 8 * 64,
        source_code(half) + 8 * 64,
        rim_code(lane),
    )
    for n, piece in enumerate(pieces):
        ref[:, n * 128 : (n + 1) * 128] = one_hot(target == piece)


def fill_pack(ref, source_code):
    t = iota((64, 256), 0)
    target = code_of((t & 31) >> 2, (t & 3) + jnp.where(t >= 32, 28, 0))
    ref[...] = one_hot(target == source_code(iota((1, 256), 1)))


class Exchange:
    def __init__(self, where, source, pack, scratch):
        self.where, self.source, self.pack = where, source, pack
        self.packed, self.north, self.south, self.rim, self.ssem, self.rsem = scratch
        self.copies = []

    def copy(self, source, target, lat, lon):
        n = len(self.copies)
        made = pltpu.make_async_remote_copy(
            src_ref=source,
            dst_ref=target,
            send_sem=self.ssem.at[n],
            recv_sem=self.rsem.at[n],
            device_id={
                "lat": lax.rem(self.where["lat"] + lat + 8, 8),
                "lon": lax.rem(self.where["lon"] + lon + 8, 8),
            },
            device_id_type=MESH,
        )
        made.start()
        self.copies.append(made)

    def begin(self):
        first, last = pl.ds(0, 32), pl.ds(32, 32)
        self.copy(self.source.at[:, :, first], self.south, -1, 0)
        self.copy(self.source.at[:, :, last], self.north, 1, 0)
        for level in range(2):
            rim = dot(self.pack[...], self.source[:, level].reshape(256, 512)).astype(jnp.bfloat16)
            self.packed[0, level] = rim[:32]
            self.packed[1, level] = rim[32:]
        self.copy(self.packed.at[0], self.rim.at[:, pl.ds(0, 32)], 0, -1)
        self.copy(self.packed.at[1], self.rim.at[:, pl.ds(32, 32)], 0, 1)
        near, far = pl.ds(0, 16), pl.ds(16, 16)
        self.copy(self.packed.at[0, :, near], self.rim.at[:, pl.ds(64, 16)], -1, -1)
        self.copy(self.packed.at[1, :, near], self.rim.at[:, pl.ds(80, 16)], -1, 1)
        self.copy(self.packed.at[0, :, far], self.rim.at[:, pl.ds(96, 16)], 1, -1)
        self.copy(self.packed.at[1, :, far], self.rim.at[:, pl.ds(112, 16)], 1, 1)

    def arrive(self):
        for made in self.copies:
            made.wait_recv()

    def gather(self, level, moves):
        cells = jnp.concatenate(
            (
                self.source[:, level].reshape(256, 512),
                self.north[:, level].reshape(128, 512),
                self.south[:, level].reshape(128, 512),
                self.rim[level],
            ),
            axis=0,
        )
        return dot(moves[...], cells)

    def drain(self):
        for made in self.copies:
            made.wait_send()


def exchange_scratch():
    bf16 = jnp.bfloat16
    return [
        pltpu.VMEM((2, 2, 32, 512), bf16),
        pltpu.VMEM((4, 2, 32, 512), bf16),
        pltpu.VMEM((4, 2, 32, 512), bf16),
        pltpu.VMEM((2, 128, 512), bf16),
        pltpu.SemaphoreType.DMA((8,)),
        pltpu.SemaphoreType.DMA((8,)),
    ]


def send(source, target, ssem, rsem, device):
    made = pltpu.make_async_remote_copy(
        src_ref=source, dst_ref=target, send_sem=ssem, recv_sem=rsem, device_id=device, device_id_type=MESH
    )
    made.start()
    return made


def block_kernel(
    shifts_ref,
    bias_ref,
    fine_ref,
    cot_ref,
    land_ref,
    gain_attn_ref,
    gain_merge_ref,
    w_qkv_hbm,
    w_proj_hbm,
    w_merge_hbm,
    w_expand_hbm,
    out_ref,
    field_ref,
    qkv_out,
    proj_out,
    mg_out,
    ex_out,
    *scratch,
):
    scratch = list(scratch)

    def take(n):
        got = scratch[:n]
        del scratch[:n]
        return got

    f32, bf16 = jnp.float32, jnp.bfloat16
    w_qkv, w_proj, w_merge, w_expand, wsem = take(5)
    to_window, to_patch, pack_patch, pack_window = take(4)
    x_patch, c_patch, normed_w, hat_w, rstd_w = take(5)
    qkv, weights, attended, branch = take(4)
    hidden, hat_m, rstd_m, merged, slope, act, gcoarse, out_patch, ghidden, gbranch = take(10)
    sib_cot, sib_act, sib_merged, sib_gcoarse, fsem, frsem = take(6)
    gbranch_w, gattended, gqkv, grolled, normed_t, attended_t, at_source = take(7)
    acc_at1, acc_at2, acc_ex, acc_mg, got_at, asem, arsem = take(7)
    exchanges = [take(6) for _ in range(4)]
    streams_scratch = [take(10) for _ in range(4)]

    where = places()
    core, lat, lon = where["core"], where["lat"], where["lon"]
    loads = []
    for n, (far, near) in enumerate(
        ((w_qkv_hbm, w_qkv), (w_proj_hbm, w_proj), (w_merge_hbm, w_merge), (w_expand_hbm, w_expand))
    ):
        made = pltpu.make_async_copy(far, near, wsem.at[n])
        made.start()
        loads.append(made)

    barrier = pltpu.get_barrier_semaphore()
    around = [(a, b) for a in (-1, 0, 1) for b in (-1, 0, 1) if (a, b) != (0, 0)]
    around += [(2, 0), (-2, 0), (0, 2), (0, -2)]
    for a, b in around:
        pl.semaphore_signal(
            barrier,
            inc=1,
            device_id={"lat": lax.rem(lat + a + 8, 8), "lon": lax.rem(lon + b + 8, 8)},
            device_id_type=MESH,
        )

    shift_lat, shift_lon = shifts_ref[0], shifts_ref[1]
    low_lat = shift_lat <= 4
    off_lat = jnp.where(low_lat, shift_lat, shift_lat - 8)
    off_lon = jnp.where(shift_lon <= 4, shift_lon, shift_lon - 8)
    offset = off_lat * 64 + off_lon

    fill_pack(pack_patch, patch_code)
    arrange_hot = one_hot(patch_code(iota((256, 256), 0)) == fine_code(iota((1, 256), 1)))
    for source, target in ((fine_ref, x_patch), (cot_ref, c_patch)):
        for level in range(2):
            target[:, level] = dot(arrange_hot, source[level]).astype(bf16).reshape(4, 64, 512)
    pl.semaphore_wait(barrier, len(around))

    first = Exchange(where, x_patch, pack_patch, exchanges[0])
    first.begin()
    factors = [send(c_patch, sib_cot, fsem.at[0], frsem.at[0], where["sibling"])]

    fill_gather(to_window, window_code, patch_code, offset)
    fill_gather(to_patch, patch_code, window_code, -offset)
    fill_pack(pack_window, window_code)

    (land_keys,) = take(1)

    def land_window(w, carry):
        key = iota((256, 128), 1)
        col_at = (32 * lon + off_lon + 8 * w + (key & 7) + 256) & 255
        land_cols = dot(land_ref[...].astype(bf16), one_hot(iota((256, 128), 0) == col_at))
        key = iota((64, 128), 1)
        row_at = (8 * lat + off_lat + ((key & 63) >> 3) + 64) & 63
        land_keys[w] = jnp.sum(jnp.where(iota((64, 128), 0) == row_at, land_cols, 0.0), axis=0, keepdims=True)
        return carry

    lax.fori_loop(0, 4, land_window, 0)

    band = jnp.where(low_lat, lat, lax.rem(lat + 7, 8))

    def region(cell):
        row = 8 * band + ((cell & 63) >> 3)
        return jnp.where(row >= 56, 1, 0) + jnp.where(row >= 64 - shift_lat, 1, 0)

    same_region = region(iota((128, 128), 0)) == region(iota((128, 128), 1))
    heads = [jnp.where(iota((1, 128), 1) >> 5 == h, 1.0, 0.0).astype(bf16) for h in range(4)]

    def head_stack(value):
        return jnp.concatenate([value * head for head in heads], axis=0)

    def head_row(stack):
        return jnp.concatenate([stack[h * 128 : (h + 1) * 128] for h in range(4)], axis=1)

    gain_attn = gain_attn_ref[...]
    first.arrive()
    for level in range(2):
        cells = first.gather(level, to_window)
        average = jnp.mean(cells, axis=-1, keepdims=True)
        centred = cells - average
        rstd = lax.rsqrt(jnp.mean(centred * centred, axis=-1, keepdims=True) + epsilon)
        hat = centred * rstd
        hat_w[:, level] = hat.reshape(4, 64, 512)
        rstd_w[:, level] = jnp.broadcast_to(rstd, (256, 128)).reshape(4, 64, 128)
        normed_w[:, level] = (hat * gain_attn).astype(bf16).reshape(4, 64, 512)

    loads[0].wait()
    normed = normed_w[...].reshape(512, 512)

    def project(n, carry):
        cols = w_qkv[:, pl.ds(pl.multiple_of(n * 256, 256), 256)]
        got = dot(normed_w[...].reshape(512, 512), cols).astype(bf16)
        for part in range(2):
            qkv[2 * n + part] = got[:, part * 128 : (part + 1) * 128].reshape(4, 128, 128)
        return carry

    lax.fori_loop(0, 6, project, 0)
    normed_t[...] = normed.T

    scale = 32.0 ** (-0.5)

    def attend(n, carry):
        w, g = n >> 2, n & 3
        scores = dot_nt(head_stack(qkv[g, w]), qkv[4 + g, w])
        land = land_keys[w]
        parts = []
        for h in range(4):
            score = scores[h * 128 : (h + 1) * 128] * scale + bias_ref[4 * g + h] * land
            score = jnp.where(same_region, score, -1000000000.0)
            raised = jnp.exp(score - jnp.max(score, axis=-1, keepdims=True))
            parts.append((raised / jnp.sum(raised, axis=-1, keepdims=True)).astype(bf16))
        weights[w, g] = jnp.concatenate(parts, axis=0)
        mixed = dot(jnp.concatenate(parts, axis=1), head_stack(qkv[8 + g, w]))
        attended[w, :, pl.ds(pl.multiple_of(g * 128, 128), 128)] = mixed.astype(bf16)
        return carry

    lax.fori_loop(0, 16, attend, 0)

    loads[1].wait()
    mixed_all = attended[...].reshape(512, 512)
    branch[...] = dot(mixed_all, w_proj[...]).astype(bf16).reshape(4, 2, 64, 512)
    second = Exchange(where, branch, pack_window, exchanges[1])
    second.begin()
    attended_t[...] = mixed_all.T
    second.arrive()
    for level in range(2):
        back = second.gather(level, to_patch).reshape(4, 64, 512)
        hidden[:, level] = (x_patch[:, level].astype(f32) + back.astype(bf16).astype(f32)).astype(bf16)

    def patches(ref):
        return jnp.concatenate([ref[q].reshape(128, 512) for q in range(4)], axis=1)

    gain_merge = gain_merge_ref[...]
    cells = patches(hidden).astype(f32)
    average = jnp.mean(cells, axis=-1, keepdims=True)
    centred = cells - average
    rstd = lax.rsqrt(jnp.mean(centred * centred, axis=-1, keepdims=True) + epsilon)
    hat = centred * rstd
    hat_m[...] = hat
    rstd_m[...] = jnp.broadcast_to(rstd, (128, 128))
    scaled = (hat * gain_merge).astype(bf16)
    for q in range(4):
        merged[q] = scaled[:, q * 512 : (q + 1) * 512]
    other = pl.multiple_of((1 - core) * 256, 256)
    factors.append(send(merged.at[:, :, pl.ds(other, 256)], sib_merged, fsem.at[1], frsem.at[1], where["sibling"]))

    loads[2].wait()
    bend = 0.7978845608028654

    def merge(n, carry):
        rows = jnp.concatenate([merged[q] for q in range(4)], axis=1)
        coarse = dot(rows, w_merge[:, pl.ds(pl.multiple_of(n * 256, 256), 256)])
        square = coarse * coarse
        bent = jnp.tanh(bend * (coarse + 0.044715 * (coarse * square)))
        act[n] = (0.5 * coarse * (1.0 + bent)).astype(bf16)
        inner = bend * (1.0 + 3.0 * 0.044715 * square)
        slope[n] = 0.5 * (1.0 + bent) + 0.5 * coarse * (1.0 - bent * bent) * inner
        return carry

    lax.fori_loop(0, 4, merge, 0)
    other = pl.multiple_of((1 - core) * 128, 128)
    factors.append(send(act.at[:, :, pl.ds(other, 128)], sib_act, fsem.at[2], frsem.at[2], where["sibling"]))

    loads[3].wait()

    def back_expand(n, carry):
        rows = patches(c_patch)
        slab = w_expand[pl.ds(pl.multiple_of(n * 256, 256), 256), :]
        gcoarse[n] = (slope[n] * dot_nt(rows, slab)).astype(bf16)
        return carry

    lax.fori_loop(0, 4, back_expand, 0)
    factors.append(send(gcoarse, sib_gcoarse, fsem.at[3], frsem.at[3], where["sibling"]))

    gc_rows = jnp.concatenate([gcoarse[n] for n in range(4)], axis=1)

    def back_merge(q, carry):
        rows = jnp.concatenate([gcoarse[n] for n in range(4)], axis=1)
        slab = w_merge[pl.ds(pl.multiple_of(q * 512, 512), 512), :]
        ghidden[q] = dot_nt(rows, slab).reshape(2, 64, 512)
        return carry

    lax.fori_loop(0, 4, back_merge, 0)
    gain = [gain_merge[:, q * 512 : (q + 1) * 512] for q in range(4)]
    first_sum = jnp.zeros((128, 1), f32)
    second_sum = jnp.zeros((128, 1), f32)
    for q in range(4):
        grad = ghidden[q].reshape(128, 512) * gain[q]
        first_sum += jnp.sum(grad, axis=-1, keepdims=True)
        second_sum += jnp.sum(grad * hat_m[:, q * 512 : (q + 1) * 512], axis=-1, keepdims=True)
    first_sum, second_sum = first_sum / 2048.0, second_sum / 2048.0
    rstd = rstd_m[:, 0:1]
    for q in range(4):
        grad = ghidden[q].reshape(128, 512) * gain[q]
        grad = rstd * (grad - first_sum - hat_m[:, q * 512 : (q + 1) * 512] * second_sum)
        grad = grad + c_patch[q].reshape(128, 512).astype(f32)
        ghidden[q] = grad.reshape(2, 64, 512)
        gbranch[q] = grad.astype(bf16).reshape(2, 64, 512)

    third = Exchange(where, gbranch, pack_patch, exchanges[2])
    third.begin()

    def store_at1(value):
        qkv_out[:, 0:1024] = value

    def store_at2(value):
        qkv_out[:, 1024:1536] = value[:, :512]
        proj_out[...] = value[:, 512:]

    def store_ex(value):
        ex_out[...] = value

    def store_mg(value):
        mg_out[...] = value

    streams = [
        Stream(where, acc_ex, "y", streams_scratch[0], store_ex),
        Stream(where, acc_mg, "x", streams_scratch[1], store_mg),
        Stream(where, acc_at1, "y", streams_scratch[2], store_at1),
        Stream(where, acc_at2, "x", streams_scratch[3], store_at2),
    ]
    for made in factors:
        made.wait_recv()

    def grad_expand(y, carry):
        left = jnp.concatenate((act[y, :, pl.ds(pl.multiple_of(core * 128, 128), 128)], sib_act[y]), axis=0).T
        for q in range(4):
            right = jnp.concatenate((c_patch[q].reshape(128, 512), sib_cot[q].reshape(128, 512)), axis=0)
            acc_ex[y, :, :, q * 512 : (q + 1) * 512] = dot(left, right).astype(bf16).reshape(4, 32, 512)
        return carry

    lax.fori_loop(0, 4, grad_expand, 0)
    streams[0].ring1.begin()

    def grad_merge(y, carry):
        left = jnp.concatenate(
            (merged[y, :, pl.ds(pl.multiple_of(core * 256, 256), 256)], sib_merged[y]), axis=0
        ).T
        for n in range(4):
            right = jnp.concatenate((gcoarse[n], sib_gcoarse[n]), axis=0)
            acc_mg[y, :, :, n * 256 : (n + 1) * 256] = dot(left, right).astype(bf16).reshape(4, 64, 256)
        return carry

    lax.fori_loop(0, 4, grad_merge, 0)
    streams[1].ring1.begin()

    third.arrive()
    for level in range(2):
        gbranch_w[:, level] = third.gather(level, to_window).astype(bf16).reshape(4, 64, 512)
    gattended[...] = dot_nt(gbranch_w[...].reshape(512, 512), w_proj[...]).astype(bf16).reshape(4, 128, 512)

    def attend_back(n, carry):
        w, g = n >> 2, n & 3
        queries, keys = head_stack(qkv[g, w]), qkv[4 + g, w]
        grads = head_stack(gattended[w, :, pl.ds(pl.multiple_of(g * 128, 128), 128)])
        grad_weights = dot_nt(grads, qkv[8 + g, w])
        weight = weights[w, g]
        wide = weight.astype(f32)
        delta = jnp.sum(wide * grad_weights, axis=-1, keepdims=True)
        grad_scores = (wide * (grad_weights - delta) * scale).astype(bf16)
        gqkv[g, w] = dot(head_row(grad_scores), head_stack(keys)).astype(bf16)
        gqkv[4 + g, w] = dot_tn(grad_scores, queries).astype(bf16)
        gqkv[8 + g, w] = dot_tn(weight, grads).astype(bf16)
        return carry

    lax.fori_loop(0, 16, attend_back, 0)
    streams[0].ring1.middle()
    streams[1].ring1.middle()

    def norm_back(half, carry):
        rows = jnp.concatenate([gqkv[n, pl.ds(2 * half, 2)].reshape(256, 128) for n in range(12)], axis=1)
        grad = dot_nt(rows, w_qkv[...]) * gain_attn
        hat = hat_w[pl.ds(2 * half, 2)].reshape(256, 512)
        rstd = rstd_w[pl.ds(2 * half, 2)].reshape(256, 128)[:, 0:1]
        first_mean = jnp.mean(grad, axis=-1, keepdims=True)
        second_mean = jnp.mean(grad * hat, axis=-1, keepdims=True)
        grad = rstd * (grad - first_mean - hat * second_mean)
        grolled[pl.ds(2 * half, 2)] = grad.astype(bf16).reshape(2, 2, 64, 512)
        return carry

    lax.fori_loop(0, 2, norm_back, 0)
    fourth = Exchange(where, grolled, pack_window, exchanges[3])
    fourth.begin()

    def grad_qkv(n, carry):
        right = jnp.concatenate([gqkv[2 * n + part].reshape(512, 128) for part in range(2)], axis=1)
        got = dot(normed_t[...], right).astype(bf16)
        at_source[:, :, :, :, pl.ds(pl.multiple_of(n * 256, 256), 256)] = got.reshape(4, 2, 4, 16, 256)
        return carry

    lax.fori_loop(0, 6, grad_qkv, 0)
    got = dot(attended_t[...], gbranch_w[...].reshape(512, 512)).astype(bf16)
    at_source[:, :, :, :, 1536:2048] = got.reshape(4, 2, 4, 16, 512)
    pair = send(at_source.at[:, 1 - core], got_at, asem.at[0], arsem.at[0], where["sibling"])
    streams[0].ring1.finish()
    streams[0].ring2.begin()
    streams[1].ring1.finish()
    streams[1].ring2.begin()

    pair.wait_recv()

    def sum_pair(n, carry):
        y, x = n // 4, lax.rem(n, 4)
        total = at_source[y, core, x].astype(f32) + got_at[y, x].astype(f32)
        acc_at1[y, x] = total[:, :1024].astype(bf16)
        acc_at2[y, x] = total[:, 1024:].astype(bf16)
        return carry

    lax.fori_loop(0, 16, sum_pair, 0)
    streams[2].ring1.begin()
    streams[3].ring1.begin()

    fine_hot = one_hot(fine_code(iota((256, 256), 0)) == patch_code(iota((1, 256), 1)))

    def expand(q, carry):
        rows = jnp.concatenate([act[n] for n in range(4)], axis=1)
        grown = dot(rows, w_expand[:, pl.ds(pl.multiple_of(q * 512, 512), 512)])
        out_patch[q] = (hidden[q].reshape(128, 512).astype(f32) + grown).astype(bf16).reshape(2, 64, 512)
        return carry

    lax.fori_loop(0, 4, expand, 0)
    for level in range(2):
        out_ref[level] = dot(fine_hot, out_patch[:, level].reshape(256, 512)).astype(bf16)

    streams[2].ring1.middle()
    streams[3].ring1.middle()
    fourth.arrive()
    for level in range(2):
        back = fourth.gather(level, to_patch).astype(bf16).astype(f32)
        total = (ghidden[:, level].reshape(256, 512) + back).astype(bf16)
        field_ref[level] = dot(fine_hot, total).astype(bf16)

    streams[0].ring2.middle()
    streams[1].ring2.middle()
    streams[2].ring1.finish()
    streams[2].ring2.begin()
    streams[3].ring1.finish()
    streams[3].ring2.begin()
    streams[0].ring2.finish()
    streams[0].z_begin()
    streams[1].ring2.finish()
    streams[1].z_begin()
    streams[2].ring2.middle()
    streams[3].ring2.middle()
    streams[2].ring2.finish()
    streams[2].z_begin()
    streams[3].ring2.finish()
    streams[3].z_begin()
    for stream in streams:
        stream.z_finish()

    for made in factors:
        made.wait_send()
    pair.wait_send()
    for each in (first, second, third, fourth):
        each.drain()
    for stream in streams:
        stream.drain()


def on_device(
    fine_field,
    cotangent,
    land_sea,
    shifts,
    gain_attn,
    w_qkv,
    w_proj,
    land_bias,
    gain_merge,
    w_merge,
    w_expand,
):
    vmem = pl.BlockSpec(memory_space=pltpu.VMEM)
    smem = pl.BlockSpec(memory_space=pltpu.SMEM)
    hbm = pl.BlockSpec(memory_space=pl.ANY)
    f32, bf16 = jnp.float32, jnp.bfloat16
    cells = (4, 2, 64, 512)
    scratch = [
        pltpu.VMEM((512, 1536), bf16),
        pltpu.VMEM((512, 512), bf16),
        pltpu.VMEM((2048, 1024), bf16),
        pltpu.VMEM((1024, 2048), bf16),
        pltpu.SemaphoreType.DMA((4,)),
        pltpu.VMEM((256, 640), bf16),
        pltpu.VMEM((256, 640), bf16),
        pltpu.VMEM((64, 256), bf16),
        pltpu.VMEM((64, 256), bf16),
        pltpu.VMEM(cells, bf16),
        pltpu.VMEM(cells, bf16),
        pltpu.VMEM(cells, bf16),
        pltpu.VMEM(cells, f32),
        pltpu.VMEM((4, 2, 64, 128), f32),
        pltpu.VMEM((12, 4, 128, 128), bf16),
        pltpu.VMEM((4, 4, 512, 128), bf16),
        pltpu.VMEM((4, 128, 512), bf16),
        pltpu.VMEM(cells, bf16),
        pltpu.VMEM(cells, bf16),
        pltpu.VMEM((128, 2048), f32),
        pltpu.VMEM((128, 128), f32),
        pltpu.VMEM((4, 128, 512), bf16),
        pltpu.VMEM((4, 128, 256), f32),
        pltpu.VMEM((4, 128, 256), bf16),
        pltpu.VMEM((4, 128, 256), bf16),
        pltpu.VMEM(cells, bf16),
        pltpu.VMEM(cells, f32),
        pltpu.VMEM(cells, bf16),
        pltpu.VMEM(cells, bf16),
        pltpu.VMEM((4, 128, 128), bf16),
        pltpu.VMEM((4, 128, 256), bf16),
        pltpu.VMEM((4, 128, 256), bf16),
        pltpu.SemaphoreType.DMA((4,)),
        pltpu.SemaphoreType.DMA((4,)),
        pltpu.VMEM(cells, bf16),
        pltpu.VMEM((4, 128, 512), bf16),
        pltpu.VMEM((12, 4, 128, 128), bf16),
        pltpu.VMEM(cells, bf16),
        pltpu.VMEM((512, 512), bf16),
        pltpu.VMEM((512, 512), bf16),
        pltpu.VMEM((4, 2, 4, 16, 2048), bf16),
        pltpu.VMEM((4, 4, 16, 1024), bf16),
        pltpu.VMEM((4, 4, 16, 1024), bf16),
        pltpu.VMEM((4, 4, 32, 2048), bf16),
        pltpu.VMEM((4, 4, 64, 1024), bf16),
        pltpu.VMEM((4, 4, 16, 2048), bf16),
        pltpu.SemaphoreType.DMA((1,)),
        pltpu.SemaphoreType.DMA((1,)),
    ]
    for _ in range(4):
        scratch += exchange_scratch()
    scratch += stream_scratch(32, 2048, bf16)
    scratch += stream_scratch(64, 1024, bf16)
    scratch += stream_scratch(16, 1024, f32)
    scratch += stream_scratch(16, 1024, f32)
    scratch += [pltpu.VMEM((4, 1, 128), f32)]
    results = pl.pallas_call(
        block_kernel,
        out_shape=(
            jax.ShapeDtypeStruct((2, 256, 512), bf16),
            jax.ShapeDtypeStruct((2, 256, 512), bf16),
            jax.ShapeDtypeStruct((8, 1536), f32),
            jax.ShapeDtypeStruct((8, 512), f32),
            jax.ShapeDtypeStruct((32, 1024), f32),
            jax.ShapeDtypeStruct((16, 2048), f32),
        ),
        in_specs=[smem, smem] + [vmem] * 5 + [hbm] * 4,
        out_specs=(vmem,) * 6,
        scratch_shapes=scratch,
        compiler_params=pltpu.CompilerParams(
            collective_id=0, has_side_effects=True, vmem_limit_bytes=60 * 2**20
        ),
        name="attention_block",
    )(
        shifts,
        land_bias,
        fine_field.reshape(2, 256, 512),
        cotangent.reshape(2, 256, 512),
        land_sea,
        gain_attn.reshape(1, 512),
        gain_merge.reshape(1, 2048),
        w_qkv,
        w_proj,
        w_merge,
        w_expand,
    )
    output, grad_field = results[0].reshape(2, 8, 32, 512), results[1].reshape(2, 8, 32, 512)
    return (output, grad_field) + tuple(results[2:])


def solution(mesh):
    return jax.shard_map(
        on_device,
        mesh=mesh,
        in_specs=(
            P("rep", "lat", "lon", None),
            P("rep", "lat", "lon", None),
            P(),
            P(),
            P(),
            P(),
            P(),
            P(),
            P(),
            P(),
            P(),
        ),
        out_specs=(
            P("rep", "lat", "lon", None),
            P("rep", "lat", "lon", None),
            P(("rep", "lat", "lon"), None),
            P(("rep", "lat", "lon"), None),
            P(("rep", "lat", "lon"), None),
            P(("rep", "lat", "lon"), None),
        ),
        check_vma=False,
    )
```

```python
import functools

import jax
import jax.numpy as jnp
from jax import lax
from jax.experimental import pallas as pl
from jax.experimental.pallas import tpu as pltpu
from jax.sharding import PartitionSpec as P

epsilon = 1e-05

MESH = pl.DeviceIdType.MESH


class Ring:
    def __init__(self, place, right, left, block, store, bufs, send_sems, recv_sems, half):
        self.place, self.right, self.left = place, right, left
        self.block, self.store = block, store
        self.bufs, self.outs = bufs[0], bufs[1]
        self.send_sems, self.recv_sems = send_sems, recv_sems
        self.half = half
        self.copies = {}

    def part(self, k, which):
        return self.block(k).at[:, :, pl.ds(which * self.half, self.half)]

    def copy(self, slot, source, target):
        made = pltpu.make_async_remote_copy(
            src_ref=source,
            dst_ref=self.bufs.at[slot],
            send_sem=self.send_sems.at[slot],
            recv_sem=self.recv_sems.at[slot],
            device_id=target,
            device_id_type=MESH,
        )
        made.start()
        self.copies[slot] = made

    def begin(self):
        ahead = lax.rem(self.place + 1, 4)
        across = lax.rem(self.place + 2, 4)
        behind = lax.rem(self.place + 3, 4)
        self.copy(0, self.part(across, 0), self.right)
        self.copy(3, self.part(across, 1), self.left)
        self.copy(1, self.part(ahead, 1), self.right)
        self.copy(4, self.part(behind, 0), self.left)

    def middle(self):
        ahead = lax.rem(self.place + 1, 4)
        behind = lax.rem(self.place + 3, 4)
        for slot, which, k, out, target in ((0, 0, ahead, 0, self.right), (3, 1, behind, 1, self.left)):
            self.copies[slot].wait_recv()

            def add(i, carry, slot=slot, which=which, k=k, out=out):
                mine = self.block(k)[i, :, pl.ds(which * self.half, self.half)]
                total = mine.astype(jnp.float32) + self.bufs[slot, i].astype(jnp.float32)
                self.outs[out, i] = total.astype(jnp.bfloat16)
                return carry

            lax.fori_loop(0, 4, add, 0)
            self.copy(2 if out == 0 else 5, self.outs.at[out], target)

    def finish(self):
        for slot in (1, 2, 4, 5):
            self.copies[slot].wait_recv()

        def add(i, carry):
            totals = []
            for which, first, second in ((0, 2, 4), (1, 5, 1)):
                mine = self.block(self.place)[i, :, pl.ds(which * self.half, self.half)]
                totals.append(
                    mine.astype(jnp.float32)
                    + self.bufs[first, i].astype(jnp.float32)
                    + self.bufs[second, i].astype(jnp.float32)
                )
            self.store(i, totals[0], totals[1])
            return carry

        lax.fori_loop(0, 4, add, 0)

    def drain(self):
        for slot in range(6):
            self.copies[slot].wait_send()


class Stream:
    def __init__(self, where, source, first_axis, paired, scratch, store):
        buf, out, red, got, ssem, rsem = scratch
        self.where, self.paired, self.store = where, paired, store
        self.red, self.got, self.ssem, self.rsem = red, got, ssem, rsem
        self.half = source.shape[3] // 2
        axes = {
            "y": (where["y"], where["up"], where["down"], lambda k: source.at[k]),
            "x": (where["x"], where["east"], where["west"], lambda k: source.at[:, k]),
        }
        self.second_axis = "x" if first_axis == "y" else "y"
        place, right, left, block = axes[first_axis]
        self.ring = Ring(place, right, left, block, self.keep, (buf, out), ssem, rsem, self.half)
        self.place = where[self.second_axis]

    def keep(self, i, first, second):
        if self.paired:
            for z in range(2):
                rows = slice(z * 8, z * 8 + 8)
                both = jnp.concatenate((first[rows], second[rows]), axis=0)
                self.red[i, z] = both.astype(jnp.bfloat16)
        else:
            self.red[i] = jnp.concatenate((first, second), axis=1).astype(jnp.bfloat16)

    def spread(self):
        where = self.where
        self.copies = []
        for n in range(1, 8 if self.paired else 4):
            d, e = (n // 2, n % 2) if self.paired else (n, 0)
            k = lax.rem(self.place + d, 4)
            block = self.red.at[k, where["z"] * (1 - e) + (1 - where["z"]) * e] if self.paired else self.red.at[k]
            if self.second_axis == "x":
                lon = lax.rem(where["lon"] + 2 * d, 8)
                target = {"lon": lon + e * (1 - 2 * where["z"])}
            else:
                target = {
                    "lat": lax.rem(where["lat"] + 2 * d, 8),
                    "lon": where["lon"] + e * (1 - 2 * where["z"]),
                }
            made = pltpu.make_async_remote_copy(
                src_ref=block,
                dst_ref=self.got.at[n - 1],
                send_sem=self.ssem.at[5 + n],
                recv_sem=self.rsem.at[5 + n],
                device_id=target,
                device_id_type=MESH,
            )
            made.start()
            self.copies.append(made)

    def end(self):
        for made in self.copies:
            made.wait_recv()
        mine = self.red[self.place, self.where["z"]] if self.paired else self.red[self.place]
        total = mine.astype(jnp.float32)
        for n in range(len(self.copies)):
            total += self.got[n].astype(jnp.float32)
        if self.paired:
            total = jnp.concatenate((total[:8], total[8:]), axis=1)
        self.store(total)

    def drain(self):
        self.ring.drain()
        for made in self.copies:
            made.wait_send()


def stream_scratch(rows, width, paired):
    half, bf16 = width // 2, jnp.bfloat16
    return [
        pltpu.VMEM((6, 4, rows, half), bf16),
        pltpu.VMEM((2, 4, rows, half), bf16),
        pltpu.VMEM((4, 2, 16, half) if paired else (4, rows, width), bf16),
        pltpu.VMEM((7, 16, half) if paired else (3, rows, width), bf16),
        pltpu.SemaphoreType.DMA((13,)),
        pltpu.SemaphoreType.DMA((13,)),
    ]


def places():
    lat, lon = lax.axis_index("lat"), lax.axis_index("lon")
    core, z = lax.rem(lat, 2), lax.rem(lon, 2)
    return {
        "lat": lat,
        "lon": lon,
        "y": lat // 2,
        "x": lon // 2,
        "core": core,
        "z": z,
        "up": {"lat": lax.rem(lat + 2, 8)},
        "down": {"lat": lax.rem(lat + 6, 8)},
        "east": {"lon": lax.rem(lon + 2, 8)},
        "west": {"lon": lax.rem(lon + 6, 8)},
        "beside": {"lon": lon + 1 - 2 * z},
        "sibling": {"lat": lat + 1 - 2 * core},
        "corner": {"lat": lat + 1 - 2 * core, "lon": lon + 1 - 2 * z},
    }


def dot(a, b):
    return lax.dot_general(a, b, (((1,), (0,)), ((), ())), preferred_element_type=jnp.float32)


def dot_nt(a, b):
    return lax.dot_general(a, b, (((1,), (1,)), ((), ())), preferred_element_type=jnp.float32)


def dot_tn(a, b):
    return lax.dot_general(a, b, (((0,), (0,)), ((), ())), preferred_element_type=jnp.float32)


def code_of(row, col):
    return (row + 16) * 64 + (col + 16)


def fine_code(s):
    return code_of(s >> 5, s & 31)


def patch_code(s):
    quarter, coarse = s >> 6, s & 63
    return code_of(2 * (coarse >> 4) + (quarter >> 1), 2 * (coarse & 15) + (quarter & 1))


def window_code(s):
    return code_of((s & 63) >> 3, 8 * (s >> 6) + (s & 7))


def rim_code(t):
    kind, c4 = t >> 5, t & 3
    row = jnp.where(kind < 2, (t & 31) >> 2, ((t & 15) >> 2) + jnp.where(kind == 2, 8, -4))
    west = jnp.where(kind < 2, kind & 1, (t >> 4) & 1)
    return code_of(row, c4 + 32 - 36 * west)


def iota(shape, axis):
    return lax.broadcasted_iota(jnp.int32, shape, axis)


def one_hot(same):
    return jnp.where(same, 1.0, 0.0).astype(jnp.bfloat16)


def fill_gather(ref, target_code, source_code, offset):
    target = target_code(iota((256, 128), 0)) + offset
    lane = iota((1, 128), 1)
    half = (lane >> 5 << 6) + (lane & 31)
    pieces = (
        source_code(lane),
        source_code(lane + 128),
        source_code(half + 32) - 8 * 64,
        source_code(half) + 8 * 64,
        rim_code(lane),
    )
    for n, piece in enumerate(pieces):
        ref[:, n * 128 : (n + 1) * 128] = one_hot(target == piece)


def fill_pack(ref, source_code):
    t = iota((64, 256), 0)
    target = code_of((t & 31) >> 2, (t & 3) + jnp.where(t >= 32, 28, 0))
    ref[...] = one_hot(target == source_code(iota((1, 256), 1)))


class Exchange:
    def __init__(self, where, source, pack, scratch):
        self.where, self.source, self.pack = where, source, pack
        self.packed, self.north, self.south, self.rim, self.ssem, self.rsem = scratch
        self.copies = []

    def make(self, n, source, target, lat, lon):
        return pltpu.make_async_remote_copy(
            src_ref=source,
            dst_ref=target,
            send_sem=self.ssem.at[n],
            recv_sem=self.rsem.at[n],
            device_id={
                "lat": lax.rem(self.where["lat"] + lat + 8, 8),
                "lon": lax.rem(self.where["lon"] + lon + 8, 8),
            },
            device_id_type=MESH,
        )

    def rows(self, quarter):
        first, last = pl.ds(0, 32), pl.ds(32, 32)
        return (
            self.make(quarter, self.source.at[quarter, :, first], self.south.at[quarter], -1, 0),
            self.make(quarter + 4, self.source.at[quarter, :, last], self.north.at[quarter], 1, 0),
        )

    def begin_rows(self, quarter):
        for made in self.rows(quarter):
            made.start()

    def begin_rim(self, quarters=(0, 1, 2, 3)):
        moves = jnp.concatenate([self.pack[:, q * 64 : (q + 1) * 64] for q in quarters], axis=1)
        for level in range(2):
            cells = jnp.concatenate([self.source[q, level] for q in quarters], axis=0)
            rim = dot(moves, cells).astype(jnp.bfloat16)
            self.packed[0, level] = rim[:32]
            self.packed[1, level] = rim[32:]
        near, far = pl.ds(0, 16), pl.ds(16, 16)
        packed, rim = self.packed, self.rim
        self.copies = [
            self.make(8, packed.at[0], rim.at[:, pl.ds(0, 32)], 0, -1),
            self.make(9, packed.at[1], rim.at[:, pl.ds(32, 32)], 0, 1),
            self.make(10, packed.at[0, :, near], rim.at[:, pl.ds(64, 16)], -1, -1),
            self.make(11, packed.at[1, :, near], rim.at[:, pl.ds(80, 16)], -1, 1),
            self.make(12, packed.at[0, :, far], rim.at[:, pl.ds(96, 16)], 1, -1),
            self.make(13, packed.at[1, :, far], rim.at[:, pl.ds(112, 16)], 1, 1),
        ]
        for made in self.copies:
            made.start()

    def begin(self):
        for quarter in range(4):
            self.begin_rows(quarter)
        self.begin_rim()

    def arrive(self):
        for quarter in range(4):
            self.copies += self.rows(quarter)
        for made in self.copies:
            made.wait_recv()

    def gather(self, level, moves):
        cells = jnp.concatenate(
            (
                self.source[:, level].reshape(256, 512),
                self.north[:, level].reshape(128, 512),
                self.south[:, level].reshape(128, 512),
                self.rim[level],
            ),
            axis=0,
        )
        return dot(moves[...], cells)

    def drain(self):
        for made in self.copies:
            made.wait_send()


def exchange_scratch():
    bf16 = jnp.bfloat16
    return [
        pltpu.VMEM((2, 2, 32, 512), bf16),
        pltpu.VMEM((4, 2, 32, 512), bf16),
        pltpu.VMEM((4, 2, 32, 512), bf16),
        pltpu.VMEM((2, 128, 512), bf16),
        pltpu.SemaphoreType.DMA((14,)),
        pltpu.SemaphoreType.DMA((14,)),
    ]


def send(source, target, ssem, rsem, device):
    made = pltpu.make_async_remote_copy(
        src_ref=source, dst_ref=target, send_sem=ssem, recv_sem=rsem, device_id=device, device_id_type=MESH
    )
    made.start()
    return made


def block_kernel(
    shifts_ref,
    bias_ref,
    fine_ref,
    cot_ref,
    land_ref,
    gain_attn_ref,
    gain_merge_ref,
    w_qkv_hbm,
    w_proj_hbm,
    w_merge_hbm,
    w_expand_hbm,
    out_ref,
    field_ref,
    qkv_out,
    proj_out,
    mg_out,
    ex_out,
    *scratch,
):
    scratch = list(scratch)

    def take(n):
        got = scratch[:n]
        del scratch[:n]
        return got

    f32, bf16 = jnp.float32, jnp.bfloat16
    w_qkv, w_proj, w_merge, w_expand, wsem = take(5)
    to_window, to_patch, pack_patch, pack_window = take(4)
    x_patch, c_patch, normed_w, hat_w, rstd_w = take(5)
    qkv, qkv_t, weights, branch = take(4)
    hidden, hat_m, rstd_m, merged, slope, act, gcoarse, out_patch, ghidden, gbranch = take(10)
    cots, gcoarses, act_t, merged_t, acts, mergeds, fsem, frsem = take(8)
    gbranch_w, gattended, gattended_t, gqkv, grolled, normed_t, attended_t = take(7)
    sib_normed, sib_attended, sib_gbranch, sib_gqkv, asem, arsem = take(6)
    acc_ex, acc_mg, acc_pj, acc_q1, acc_q2 = take(5)
    exchanges = [take(6) for _ in range(4)]
    streams_scratch = [take(6) for _ in range(5)]

    where = places()
    core, lat, lon = where["core"], where["lat"], where["lon"]
    loads = []
    for n, (far, near) in enumerate(
        ((w_qkv_hbm, w_qkv), (w_proj_hbm, w_proj), (w_merge_hbm, w_merge), (w_expand_hbm, w_expand))
    ):
        made = pltpu.make_async_copy(far, near, wsem.at[n])
        made.start()
        loads.append(made)

    barrier = pltpu.get_barrier_semaphore()
    beside = lon + 1 - 2 * where["z"]
    around = [(lat + a, lon + b) for a in (7, 8, 9) for b in (7, 8, 9) if (a, b) != (8, 8)]
    around += [(lat, lon + b) for b in range(2, 7)] + [(lat + a, lon) for a in (2, 4, 6)]
    around += [(lat + a, beside) for a in (2, 4, 6)]
    for a, b in around:
        pl.semaphore_signal(
            barrier, inc=1, device_id={"lat": lax.rem(a, 8), "lon": lax.rem(b, 8)}, device_id_type=MESH
        )

    shift_lat, shift_lon = shifts_ref[0], shifts_ref[1]
    low_lat = shift_lat <= 4
    off_lat = jnp.where(low_lat, shift_lat, shift_lat - 8)
    off_lon = jnp.where(shift_lon <= 4, shift_lon, shift_lon - 8)
    offset = off_lat * 64 + off_lon

    fill_pack(pack_patch, patch_code)
    arrange_hot = one_hot(patch_code(iota((256, 256), 0)) == fine_code(iota((1, 256), 1)))
    for source, target in ((fine_ref, x_patch), (cot_ref, c_patch)):
        for level in range(2):
            target[:, level] = dot(arrange_hot, source[level]).astype(bf16).reshape(4, 64, 512)
    pl.semaphore_wait(barrier, len(around))

    first = Exchange(where, x_patch, pack_patch, exchanges[0])
    first.begin()
    sent = []

    def share(n, source, target, name):
        made = send(source, target, fsem.at[n], frsem.at[n], where[name])
        sent.append(made)
        return made

    cot_side = share(0, c_patch, cots.at[0], "sibling")
    cot_beside = share(1, c_patch, cots.at[1], "beside")

    fill_gather(to_window, window_code, patch_code, offset)
    fill_gather(to_patch, patch_code, window_code, -offset)
    fill_pack(pack_window, window_code)

    (land_keys,) = take(1)

    def land_window(w, carry):
        key = iota((128, 256), 0)
        col_at = (32 * lon + off_lon + 8 * w + (key & 7) + 256) & 255
        land_rows = dot_nt(one_hot(iota((128, 256), 1) == col_at), land_ref[...].astype(bf16))
        row_at = (8 * lat + off_lat + ((iota((128, 64), 0) & 63) >> 3) + 64) & 63
        land = jnp.sum(jnp.where(iota((128, 64), 1) == row_at, land_rows, 0.0), axis=1, keepdims=True)
        land_keys[w] = jnp.broadcast_to(land, (128, 128))
        return carry

    lax.fori_loop(0, 4, land_window, 0)

    band = jnp.where(low_lat, lat, lax.rem(lat + 7, 8))

    def region(cell):
        row = 8 * band + ((cell & 63) >> 3)
        return jnp.where(row >= 56, 1, 0) + jnp.where(row >= 64 - shift_lat, 1, 0)

    same_region = region(iota((128, 128), 0)) == region(iota((128, 128), 1))
    heads = [jnp.where(iota((1, 128), 1) >> 5 == h, 1.0, 0.0).astype(bf16) for h in range(4)]

    def head_stack(value):
        return jnp.concatenate([value * head for head in heads], axis=0)

    def head_blocks(value):
        blocks = []
        for h in range(4):
            pieces = [value[32 * h : 32 * h + 32]]
            if h > 0:
                pieces.insert(0, jnp.zeros((32 * h, 128), bf16))
            if h < 3:
                pieces.append(jnp.zeros((96 - 32 * h, 128), bf16))
            blocks.append(jnp.concatenate(pieces, axis=0))
        return jnp.concatenate(blocks, axis=1)

    def under(value):
        return jnp.concatenate([value[:, h * 128 : (h + 1) * 128] for h in range(4)], axis=0)

    gain_attn = gain_attn_ref[...]
    first.arrive()
    for level in range(2):
        cells = first.gather(level, to_window)
        average = jnp.mean(cells, axis=-1, keepdims=True)
        centred = cells - average
        rstd = lax.rsqrt(jnp.mean(centred * centred, axis=-1, keepdims=True) + epsilon)
        hat = centred * rstd
        hat_w[:, level] = hat.reshape(4, 64, 512)
        rstd_w[:, level] = jnp.broadcast_to(rstd, (256, 128)).reshape(4, 64, 128)
        normed_w[:, level] = (hat * gain_attn).astype(bf16).reshape(4, 64, 512)

    loads[0].wait()
    normed = normed_w[...].reshape(512, 512)

    def project(n, carry):
        cols = w_qkv[:, pl.ds(pl.multiple_of(n * 256, 256), 256)]
        got = dot(normed_w[...].reshape(512, 512), cols).astype(bf16)
        for part in range(2):
            piece = got[:, part * 128 : (part + 1) * 128]
            qkv[2 * n + part] = piece.reshape(4, 128, 128)
            turned = piece.T
            for w in range(4):
                qkv_t[2 * n + part, w] = turned[:, w * 128 : (w + 1) * 128]
        return carry

    lax.fori_loop(0, 6, project, 0)
    normed_t[...] = normed.T.reshape(4, 2, 64, 512)
    pairs = [send(normed_t.at[:, 1 - core], sib_normed, asem.at[0], arsem.at[0], where["sibling"])]

    scale = 32.0 ** (-0.5)

    def attend(w, g):
        scores = dot(qkv[4 + g, w], head_blocks(qkv_t[g, w]))
        parts = []
        for h in range(4):
            score = scores[:, h * 128 : (h + 1) * 128] * scale + bias_ref[4 * g + h] * land_keys[w]
            score = jnp.where(same_region, score, -1000000000.0)
            raised = jnp.exp(score - jnp.max(score, axis=0, keepdims=True))
            parts.append((raised * (1.0 / jnp.sum(raised, axis=0, keepdims=True))).astype(bf16))
        weights[w, g] = jnp.concatenate(parts, axis=1)
        mixed = dot(head_blocks(qkv_t[8 + g, w]), jnp.concatenate(parts, axis=0))
        attended_t[g, :, :, pl.ds(pl.multiple_of(w * 128, 128), 128)] = mixed.astype(bf16).reshape(2, 64, 128)

    second = Exchange(where, branch, pack_window, exchanges[1])

    def attend_window(n, carry):
        w = lax.rem(3 * n, 4)
        for g in range(4):
            attend(w, g)
        mixed = attended_t[:, :, :, pl.ds(pl.multiple_of(w * 128, 128), 128)].reshape(512, 128).T
        branch[w] = dot(mixed, w_proj[...]).astype(bf16).reshape(2, 64, 512)
        second.begin_rows(w)
        return carry

    loads[1].wait()
    lax.fori_loop(0, 2, attend_window, 0)
    second.begin_rim((0, 3))
    lax.fori_loop(2, 4, attend_window, 0)
    pairs.append(send(attended_t.at[:, 1 - core], sib_attended, asem.at[1], arsem.at[1], where["sibling"]))
    cot_beside.wait_recv()
    cot_corner = share(2, cots.at[1], cots.at[2], "sibling")
    second.arrive()
    for level in range(2):
        back = second.gather(level, to_patch).reshape(4, 64, 512)
        hidden[:, level] = (x_patch[:, level].astype(f32) + back.astype(bf16).astype(f32)).astype(bf16)

    def patches(ref):
        return jnp.concatenate([ref[q].reshape(128, 512) for q in range(4)], axis=1)

    gain_merge = gain_merge_ref[...]
    cells = patches(hidden).astype(f32)
    average = jnp.mean(cells, axis=-1, keepdims=True)
    centred = cells - average
    rstd = lax.rsqrt(jnp.mean(centred * centred, axis=-1, keepdims=True) + epsilon)
    hat = centred * rstd
    hat_m[...] = hat
    rstd_m[...] = jnp.broadcast_to(rstd, (128, 128))
    scaled = (hat * gain_merge).astype(bf16)
    for q in range(4):
        merged[q] = scaled[:, q * 512 : (q + 1) * 512]

    def part_rows(target, y, value, deep):
        value = value.T.reshape(2, 4, 2, deep, 128)
        for c in range(2):
            for z in range(2):
                target[c, z, y] = value[c, :, z]

    for q in range(4):
        part_rows(merged_t, q, scaled[:, q * 512 : (q + 1) * 512], 32)
    side, level_z = 1 - core, where["z"]
    merged_parts = [
        share(3, merged_t.at[side, level_z], mergeds.at[0], "sibling"),
        share(4, merged_t.at[core, 1 - level_z], mergeds.at[1], "beside"),
        share(5, merged_t.at[side, 1 - level_z], mergeds.at[2], "corner"),
    ]

    loads[2].wait()
    bend = 0.7978845608028654

    def merge(n, carry):
        rows = jnp.concatenate([merged[q] for q in range(4)], axis=1)
        coarse = dot(rows, w_merge[:, pl.ds(pl.multiple_of(n * 256, 256), 256)])
        square = coarse * coarse
        bent = jnp.tanh(bend * (coarse + 0.044715 * (coarse * square)))
        active = (0.5 * coarse * (1.0 + bent)).astype(bf16)
        act[n] = active
        part_rows(act_t, n, active, 16)
        inner = bend * (1.0 + 3.0 * 0.044715 * square)
        slope[n] = 0.5 * (1.0 + bent) + 0.5 * coarse * (1.0 - bent * bent) * inner
        return carry

    lax.fori_loop(0, 4, merge, 0)
    act_parts = [
        share(6, act_t.at[side, level_z], acts.at[0], "sibling"),
        share(7, act_t.at[core, 1 - level_z], acts.at[1], "beside"),
        share(8, act_t.at[side, 1 - level_z], acts.at[2], "corner"),
    ]

    loads[3].wait()

    def back_expand(n, carry):
        rows = patches(c_patch)
        slab = w_expand[pl.ds(pl.multiple_of(n * 256, 256), 256), :]
        gcoarse[n] = (slope[n] * dot_nt(rows, slab)).astype(bf16)
        return carry

    lax.fori_loop(0, 4, back_expand, 0)
    gcoarse_side = share(9, gcoarse, gcoarses.at[0], "sibling")
    gcoarse_beside = share(10, gcoarse, gcoarses.at[1], "beside")

    def store_q1(value):
        qkv_out[:, 0:768] = value

    def store_q2(value):
        qkv_out[:, 768:1536] = value

    def store_pj(value):
        proj_out[...] = value

    def store_ex(value):
        ex_out[...] = value

    def store_mg(value):
        mg_out[...] = value

    stream_ex = Stream(where, acc_ex, "x", False, streams_scratch[0], store_ex)
    stream_mg = Stream(where, acc_mg, "y", False, streams_scratch[1], store_mg)
    stream_pj = Stream(where, acc_pj, "x", True, streams_scratch[2], store_pj)
    stream_q1 = Stream(where, acc_q1, "y", True, streams_scratch[3], store_q1)
    stream_q2 = Stream(where, acc_q2, "x", True, streams_scratch[4], store_q2)
    for made in act_parts:
        made.wait_recv()
    cot_side.wait_recv()
    cot_corner.wait_recv()

    def grad_expand(q, carry):
        parts = [act_t[core, level_z]] + [acts[n] for n in range(3)]
        left = jnp.concatenate([part.reshape(256, 128) for part in parts], axis=1)
        parts = [c_patch[q]] + [cots[n, q] for n in range(3)]
        right = jnp.concatenate([part.reshape(128, 512) for part in parts], axis=0)
        got = dot(left, right).astype(bf16).reshape(4, 4, 16, 512)
        acc_ex[:, :, :, pl.ds(pl.multiple_of(q * 512, 512), 512)] = got
        return carry

    lax.fori_loop(0, 4, grad_expand, 0)
    stream_ex.ring.begin()

    def back_merge(q, carry):
        rows = jnp.concatenate([gcoarse[n] for n in range(4)], axis=1)
        slab = w_merge[pl.ds(pl.multiple_of(q * 512, 512), 512), :]
        ghidden[q] = dot_nt(rows, slab).reshape(2, 64, 512)
        return carry

    lax.fori_loop(0, 4, back_merge, 0)
    gain = [gain_merge[:, q * 512 : (q + 1) * 512] for q in range(4)]
    first_sum = jnp.zeros((128, 1), f32)
    second_sum = jnp.zeros((128, 1), f32)
    for q in range(4):
        grad = ghidden[q].reshape(128, 512) * gain[q]
        first_sum += jnp.sum(grad, axis=-1, keepdims=True)
        second_sum += jnp.sum(grad * hat_m[:, q * 512 : (q + 1) * 512], axis=-1, keepdims=True)
    first_sum, second_sum = first_sum / 2048.0, second_sum / 2048.0
    rstd = rstd_m[:, 0:1]
    for q in range(4):
        grad = ghidden[q].reshape(128, 512) * gain[q]
        grad = rstd * (grad - first_sum - hat_m[:, q * 512 : (q + 1) * 512] * second_sum)
        grad = grad + c_patch[q].reshape(128, 512).astype(f32)
        ghidden[q] = grad.reshape(2, 64, 512)
        gbranch[q] = grad.astype(bf16).reshape(2, 64, 512)

    third = Exchange(where, gbranch, pack_patch, exchanges[2])
    third.begin()

    gcoarse_beside.wait_recv()
    gcoarse_corner = share(11, gcoarses.at[1], gcoarses.at[2], "sibling")
    for made in merged_parts:
        made.wait_recv()
    gcoarse_side.wait_recv()
    gcoarse_corner.wait_recv()

    def grad_merge(n, carry):
        parts = [merged_t[core, level_z]] + [mergeds[k] for k in range(3)]
        left = jnp.concatenate([part.reshape(512, 128) for part in parts], axis=1)
        right = jnp.concatenate([gcoarse[n]] + [gcoarses[k, n] for k in range(3)], axis=0)
        got = dot(left, right).astype(bf16).reshape(4, 4, 32, 256)
        acc_mg[:, :, :, pl.ds(pl.multiple_of(n * 256, 256), 256)] = got
        return carry

    lax.fori_loop(0, 4, grad_merge, 0)
    stream_mg.ring.begin()

    third.arrive()
    for level in range(2):
        gbranch_w[:, level] = third.gather(level, to_window).astype(bf16).reshape(4, 64, 512)
    grads_w = gbranch_w[...].reshape(512, 512)
    gattended[...] = dot_nt(grads_w, w_proj[...]).astype(bf16).reshape(4, 128, 512)
    turned = dot_nt(w_proj[...], grads_w).astype(bf16)
    for w in range(4):
        gattended_t[w] = turned[:, w * 128 : (w + 1) * 128].reshape(4, 128, 128)
    pairs.append(send(gbranch_w, sib_gbranch, asem.at[2], arsem.at[2], where["sibling"]))
    stream_ex.ring.middle()

    def share_window(w):
        return pltpu.make_async_remote_copy(
            src_ref=gqkv.at[:, w],
            dst_ref=sib_gqkv.at[:, w],
            send_sem=asem.at[3 + w],
            recv_sem=arsem.at[3 + w],
            device_id=where["sibling"],
            device_id_type=MESH,
        )

    def attend_back(w, g):
        grads = gattended[w, :, g * 128 : (g + 1) * 128]
        grad_weights = dot(qkv[8 + g, w], head_blocks(gattended_t[w, g]))
        weight = weights[w, g]
        wide = weight.astype(f32)
        shared = wide * grad_weights
        delta = jnp.sum(shared, axis=0, keepdims=True)
        grad_scores = ((shared - wide * delta) * scale).astype(bf16)
        turned = dot(head_blocks(qkv_t[4 + g, w]), under(grad_scores))
        gqkv[g, w] = turned.astype(bf16).T
        gqkv[4 + g, w] = dot(grad_scores, head_stack(qkv[g, w])).astype(bf16)
        gqkv[8 + g, w] = dot(weight, head_stack(grads)).astype(bf16)

    def attend_back_window(w, carry):
        for g in range(4):
            attend_back(w, g)
        share_window(w).start()
        return carry

    lax.fori_loop(0, 2, attend_back_window, 0)
    for made in pairs:
        made.wait_recv()
    left = jnp.concatenate((attended_t[:, core].reshape(256, 512), sib_attended[...].reshape(256, 512)), axis=1)
    right = jnp.concatenate((gbranch_w[...].reshape(512, 512), sib_gbranch[...].reshape(512, 512)), axis=0)
    acc_pj[...] = dot(left, right).astype(bf16).reshape(4, 4, 16, 512)
    stream_pj.ring.begin()
    stream_mg.ring.middle()
    stream_ex.ring.finish()
    stream_ex.spread()
    lax.fori_loop(2, 4, attend_back_window, 0)
    windows = [share_window(w) for w in range(4)]
    for made in windows:
        made.wait_recv()

    def grad_qkv(target, base, n, carry):
        left = jnp.concatenate((normed_t[:, core].reshape(256, 512), sib_normed[...].reshape(256, 512)), axis=1)
        k = 2 * n + base
        own = [gqkv[k + part].reshape(512, 128) for part in range(2)]
        far = [sib_gqkv[k + part].reshape(512, 128) for part in range(2)]
        right = jnp.concatenate((jnp.concatenate(own, axis=1), jnp.concatenate(far, axis=1)), axis=0)
        got = dot(left, right).astype(bf16).reshape(4, 4, 16, 256)
        target[:, :, :, pl.ds(pl.multiple_of(n * 256, 256), 256)] = got
        return carry

    lax.fori_loop(0, 3, functools.partial(grad_qkv, acc_q1, 0), 0)
    stream_q1.ring.begin()
    lax.fori_loop(0, 3, functools.partial(grad_qkv, acc_q2, 6), 0)
    stream_q2.ring.begin()

    def norm_back(half, carry):
        rows = jnp.concatenate([gqkv[n, pl.ds(2 * half, 2)].reshape(256, 128) for n in range(12)], axis=1)
        grad = dot_nt(rows, w_qkv[...]) * gain_attn
        hat = hat_w[pl.ds(2 * half, 2)].reshape(256, 512)
        rstd = rstd_w[pl.ds(2 * half, 2)].reshape(256, 128)[:, 0:1]
        first_mean = jnp.mean(grad, axis=-1, keepdims=True)
        second_mean = jnp.mean(grad * hat, axis=-1, keepdims=True)
        grad = rstd * (grad - first_mean - hat * second_mean)
        grolled[pl.ds(2 * half, 2)] = grad.astype(bf16).reshape(2, 2, 64, 512)
        return carry

    lax.fori_loop(0, 2, norm_back, 0)
    fourth = Exchange(where, grolled, pack_window, exchanges[3])
    fourth.begin()
    stream_mg.ring.finish()
    stream_mg.spread()
    stream_pj.ring.middle()
    stream_q1.ring.middle()
    stream_q2.ring.middle()

    fine_hot = one_hot(fine_code(iota((256, 256), 0)) == patch_code(iota((1, 256), 1)))

    def expand(q, carry):
        rows = jnp.concatenate([act[n] for n in range(4)], axis=1)
        grown = dot(rows, w_expand[:, pl.ds(pl.multiple_of(q * 512, 512), 512)])
        out_patch[q] = (hidden[q].reshape(128, 512).astype(f32) + grown).astype(bf16).reshape(2, 64, 512)
        return carry

    lax.fori_loop(0, 4, expand, 0)
    for level in range(2):
        out_ref[level] = dot(fine_hot, out_patch[:, level].reshape(256, 512)).astype(bf16)

    stream_pj.ring.finish()
    stream_pj.spread()
    stream_q1.ring.finish()
    stream_q1.spread()
    stream_q2.ring.finish()
    stream_q2.spread()
    fourth.arrive()
    for level in range(2):
        back = fourth.gather(level, to_patch).astype(bf16).astype(f32)
        total = (ghidden[:, level].reshape(256, 512) + back).astype(bf16)
        field_ref[level] = dot(fine_hot, total).astype(bf16)

    streams = (stream_ex, stream_mg, stream_pj, stream_q1, stream_q2)
    for stream in streams:
        stream.end()

    for made in sent + pairs + windows:
        made.wait_send()
    for each in (first, second, third, fourth):
        each.drain()
    for stream in streams:
        stream.drain()


def deliver_kernel(*refs):
    sources, targets, held, sems = refs[:6], refs[6:12], refs[12:18], refs[18]
    loads = [pltpu.make_async_copy(a, b, sems.at[0, n]) for n, (a, b) in enumerate(zip(sources, held))]
    stores = [pltpu.make_async_copy(a, b, sems.at[1, n]) for n, (a, b) in enumerate(zip(held, targets))]
    for made in loads:
        made.start()
    for load, store in zip(loads, stores):
        load.wait()
        store.start()
    for made in stores:
        made.wait()


def deliver(results):
    hbm = pl.BlockSpec(memory_space=pl.ANY)
    return pl.pallas_call(
        deliver_kernel,
        out_shape=tuple(jax.ShapeDtypeStruct(r.shape, r.dtype) for r in results),
        in_specs=[hbm] * 6,
        out_specs=(hbm,) * 6,
        scratch_shapes=[pltpu.VMEM(r.shape, r.dtype) for r in results] + [pltpu.SemaphoreType.DMA((2, 6))],
        name="deliver",
    )(*results)


def on_device(
    fine_field,
    cotangent,
    land_sea,
    shifts,
    gain_attn,
    w_qkv,
    w_proj,
    land_bias,
    gain_merge,
    w_merge,
    w_expand,
):
    vmem = pl.BlockSpec(memory_space=pltpu.VMEM)
    smem = pl.BlockSpec(memory_space=pltpu.SMEM)
    hbm = pl.BlockSpec(memory_space=pl.ANY)
    f32, bf16 = jnp.float32, jnp.bfloat16
    cells = (4, 2, 64, 512)
    scratch = [
        pltpu.VMEM((512, 1536), bf16),
        pltpu.VMEM((512, 512), bf16),
        pltpu.VMEM((2048, 1024), bf16),
        pltpu.VMEM((1024, 2048), bf16),
        pltpu.SemaphoreType.DMA((4,)),
        pltpu.VMEM((256, 640), bf16),
        pltpu.VMEM((256, 640), bf16),
        pltpu.VMEM((64, 256), bf16),
        pltpu.VMEM((64, 256), bf16),
        pltpu.VMEM(cells, bf16),
        pltpu.VMEM(cells, bf16),
        pltpu.VMEM(cells, bf16),
        pltpu.VMEM(cells, f32),
        pltpu.VMEM((4, 2, 64, 128), f32),
        pltpu.VMEM((12, 4, 128, 128), bf16),
        pltpu.VMEM((12, 4, 128, 128), bf16),
        pltpu.VMEM((4, 4, 128, 512), bf16),
        pltpu.VMEM(cells, bf16),
        pltpu.VMEM(cells, bf16),
        pltpu.VMEM((128, 2048), f32),
        pltpu.VMEM((128, 128), f32),
        pltpu.VMEM((4, 128, 512), bf16),
        pltpu.VMEM((4, 128, 256), f32),
        pltpu.VMEM((4, 128, 256), bf16),
        pltpu.VMEM((4, 128, 256), bf16),
        pltpu.VMEM(cells, bf16),
        pltpu.VMEM(cells, f32),
        pltpu.VMEM(cells, bf16),
        pltpu.VMEM((3,) + cells, bf16),
        pltpu.VMEM((3, 4, 128, 256), bf16),
        pltpu.VMEM((2, 2, 4, 4, 16, 128), bf16),
        pltpu.VMEM((2, 2, 4, 4, 32, 128), bf16),
        pltpu.VMEM((3, 4, 4, 16, 128), bf16),
        pltpu.VMEM((3, 4, 4, 32, 128), bf16),
        pltpu.SemaphoreType.DMA((12,)),
        pltpu.SemaphoreType.DMA((12,)),
        pltpu.VMEM(cells, bf16),
        pltpu.VMEM((4, 128, 512), bf16),
        pltpu.VMEM((4, 4, 128, 128), bf16),
        pltpu.VMEM((12, 4, 128, 128), bf16),
        pltpu.VMEM(cells, bf16),
        pltpu.VMEM(cells, bf16),
        pltpu.VMEM(cells, bf16),
        pltpu.VMEM((4, 64, 512), bf16),
        pltpu.VMEM((4, 64, 512), bf16),
        pltpu.VMEM(cells, bf16),
        pltpu.VMEM((12, 4, 128, 128), bf16),
        pltpu.SemaphoreType.DMA((7,)),
        pltpu.SemaphoreType.DMA((7,)),
        pltpu.VMEM((4, 4, 16, 2048), bf16),
        pltpu.VMEM((4, 4, 32, 1024), bf16),
        pltpu.VMEM((4, 4, 16, 512), bf16),
        pltpu.VMEM((4, 4, 16, 768), bf16),
        pltpu.VMEM((4, 4, 16, 768), bf16),
    ]
    for _ in range(4):
        scratch += exchange_scratch()
    scratch += stream_scratch(16, 2048, False)
    scratch += stream_scratch(32, 1024, False)
    scratch += stream_scratch(16, 512, True)
    scratch += stream_scratch(16, 768, True)
    scratch += stream_scratch(16, 768, True)
    scratch += [pltpu.VMEM((4, 128, 128), f32)]
    results = pl.pallas_call(
        block_kernel,
        out_shape=(
            jax.ShapeDtypeStruct((2, 256, 512), bf16),
            jax.ShapeDtypeStruct((2, 256, 512), bf16),
            jax.ShapeDtypeStruct((8, 1536), f32),
            jax.ShapeDtypeStruct((8, 512), f32),
            jax.ShapeDtypeStruct((32, 1024), f32),
            jax.ShapeDtypeStruct((16, 2048), f32),
        ),
        in_specs=[smem, smem] + [vmem] * 5 + [hbm] * 4,
        out_specs=(vmem,) * 6,
        scratch_shapes=scratch,
        compiler_params=pltpu.CompilerParams(
            collective_id=0, has_side_effects=True, vmem_limit_bytes=60 * 2**20
        ),
        name="attention_block",
    )(
        shifts,
        land_bias,
        fine_field.reshape(2, 256, 512),
        cotangent.reshape(2, 256, 512),
        land_sea,
        gain_attn.reshape(1, 512),
        gain_merge.reshape(1, 2048),
        w_qkv,
        w_proj,
        w_merge,
        w_expand,
    )
    results = deliver(results)
    output, grad_field = results[0].reshape(2, 8, 32, 512), results[1].reshape(2, 8, 32, 512)
    return (output, grad_field) + tuple(results[2:])


def solution(mesh):
    return jax.shard_map(
        on_device,
        mesh=mesh,
        in_specs=(
            P("rep", "lat", "lon", None),
            P("rep", "lat", "lon", None),
            P(),
            P(),
            P(),
            P(),
            P(),
            P(),
            P(),
            P(),
            P(),
        ),
        out_specs=(
            P("rep", "lat", "lon", None),
            P("rep", "lat", "lon", None),
            P(("rep", "lat", "lon"), None),
            P(("rep", "lat", "lon"), None),
            P(("rep", "lat", "lon"), None),
            P(("rep", "lat", "lon"), None),
        ),
        check_vma=False,
    )
```

```python
import functools

import jax
import jax.numpy as jnp
from jax import lax
from jax.experimental import pallas as pl
from jax.experimental.pallas import tpu as pltpu
from jax.sharding import PartitionSpec as P

epsilon = 1e-05

MESH = pl.DeviceIdType.MESH


class Ring:
    def __init__(self, place, right, left, block, store, bufs, send_sems, recv_sems, half):
        self.place, self.right, self.left = place, right, left
        self.block, self.store = block, store
        self.bufs, self.outs = bufs[0], bufs[1]
        self.send_sems, self.recv_sems = send_sems, recv_sems
        self.half = half
        self.copies = {}

    def part(self, k, which):
        return self.block(k).at[:, :, pl.ds(which * self.half, self.half)]

    def copy(self, slot, source, target):
        made = pltpu.make_async_remote_copy(
            src_ref=source,
            dst_ref=self.bufs.at[slot],
            send_sem=self.send_sems.at[slot],
            recv_sem=self.recv_sems.at[slot],
            device_id=target,
            device_id_type=MESH,
        )
        made.start()
        self.copies[slot] = made

    def begin(self):
        ahead = lax.rem(self.place + 1, 4)
        across = lax.rem(self.place + 2, 4)
        behind = lax.rem(self.place + 3, 4)
        self.copy(0, self.part(across, 0), self.right)
        self.copy(3, self.part(across, 1), self.left)
        self.copy(1, self.part(ahead, 1), self.right)
        self.copy(4, self.part(behind, 0), self.left)

    def middle(self):
        ahead = lax.rem(self.place + 1, 4)
        behind = lax.rem(self.place + 3, 4)
        for slot, which, k, out, target in ((0, 0, ahead, 0, self.right), (3, 1, behind, 1, self.left)):
            self.copies[slot].wait_recv()

            def add(i, carry, slot=slot, which=which, k=k, out=out):
                mine = self.block(k)[i, :, pl.ds(which * self.half, self.half)]
                total = mine.astype(jnp.float32) + self.bufs[slot, i].astype(jnp.float32)
                self.outs[out, i] = total.astype(jnp.bfloat16)
                return carry

            lax.fori_loop(0, 4, add, 0)
            self.copy(2 if out == 0 else 5, self.outs.at[out], target)

    def finish(self):
        for slot in (1, 2, 4, 5):
            self.copies[slot].wait_recv()

        def add(i, carry):
            totals = []
            for which, first, second in ((0, 2, 4), (1, 5, 1)):
                mine = self.block(self.place)[i, :, pl.ds(which * self.half, self.half)]
                totals.append(
                    mine.astype(jnp.float32)
                    + self.bufs[first, i].astype(jnp.float32)
                    + self.bufs[second, i].astype(jnp.float32)
                )
            self.store(i, totals[0], totals[1])
            return carry

        lax.fori_loop(0, 4, add, 0)

    def drain(self):
        for slot in range(6):
            self.copies[slot].wait_send()


class Stream:
    def __init__(self, where, source, first_axis, paired, scratch, store):
        buf, out, red, got, ssem, rsem = scratch
        self.where, self.paired, self.store = where, paired, store
        self.red, self.got, self.ssem, self.rsem = red, got, ssem, rsem
        self.half, self.deep = source.shape[3] // 2, source.shape[2] // 2
        axes = {
            "y": (where["y"], where["up"], where["down"], lambda k: source.at[k]),
            "x": (where["x"], where["east"], where["west"], lambda k: source.at[:, k]),
        }
        self.second_axis = "x" if first_axis == "y" else "y"
        place, right, left, block = axes[first_axis]
        self.ring = Ring(place, right, left, block, self.keep, (buf, out), ssem, rsem, self.half)
        self.place = where[self.second_axis]

    def keep(self, i, first, second):
        if self.paired:
            for z in range(2):
                rows = slice(z * self.deep, (z + 1) * self.deep)
                both = jnp.concatenate((first[rows], second[rows]), axis=0 if self.deep == 8 else 1)
                self.red[i, z] = both.astype(jnp.bfloat16)
        else:
            self.red[i] = jnp.concatenate((first, second), axis=1).astype(jnp.bfloat16)

    def spread(self):
        where = self.where
        self.copies = []
        for n in range(1, 8 if self.paired else 4):
            d, e = (n // 2, n % 2) if self.paired else (n, 0)
            k = lax.rem(self.place + d, 4)
            block = self.red.at[k, where["z"] * (1 - e) + (1 - where["z"]) * e] if self.paired else self.red.at[k]
            if self.second_axis == "x":
                lon = lax.rem(where["lon"] + 2 * d, 8)
                target = {"lon": lon + e * (1 - 2 * where["z"])}
            else:
                target = {
                    "lat": lax.rem(where["lat"] + 2 * d, 8),
                    "lon": where["lon"] + e * (1 - 2 * where["z"]),
                }
            made = pltpu.make_async_remote_copy(
                src_ref=block,
                dst_ref=self.got.at[n - 1],
                send_sem=self.ssem.at[5 + n],
                recv_sem=self.rsem.at[5 + n],
                device_id=target,
                device_id_type=MESH,
            )
            made.start()
            self.copies.append(made)

    def end(self):
        for made in self.copies:
            made.wait_recv()
        mine = self.red[self.place, self.where["z"]] if self.paired else self.red[self.place]
        total = mine.astype(jnp.float32)
        for n in range(len(self.copies)):
            total += self.got[n].astype(jnp.float32)
        if self.paired and self.deep == 8:
            total = jnp.concatenate((total[:8], total[8:]), axis=1)
        self.store(total)

    def drain(self):
        self.ring.drain()
        for made in self.copies:
            made.wait_send()


def stream_scratch(rows, width, paired):
    half, bf16 = width // 2, jnp.bfloat16
    block = (16, half) if rows == 16 else (rows // 2, width)
    return [
        pltpu.VMEM((6, 4, rows, half), bf16),
        pltpu.VMEM((2, 4, rows, half), bf16),
        pltpu.VMEM((4, 2) + block if paired else (4, rows, width), bf16),
        pltpu.VMEM((7,) + block if paired else (3, rows, width), bf16),
        pltpu.SemaphoreType.DMA((13,)),
        pltpu.SemaphoreType.DMA((13,)),
    ]


def places():
    lat, lon = lax.axis_index("lat"), lax.axis_index("lon")
    core, z = lax.rem(lat, 2), lax.rem(lon, 2)
    return {
        "lat": lat,
        "lon": lon,
        "y": lat // 2,
        "x": lon // 2,
        "core": core,
        "z": z,
        "up": {"lat": lax.rem(lat + 2, 8)},
        "down": {"lat": lax.rem(lat + 6, 8)},
        "east": {"lon": lax.rem(lon + 2, 8)},
        "west": {"lon": lax.rem(lon + 6, 8)},
        "beside": {"lon": lon + 1 - 2 * z},
        "sibling": {"lat": lat + 1 - 2 * core},
        "corner": {"lat": lat + 1 - 2 * core, "lon": lon + 1 - 2 * z},
    }


def dot(a, b):
    return lax.dot_general(a, b, (((1,), (0,)), ((), ())), preferred_element_type=jnp.float32)


def dot_nt(a, b):
    return lax.dot_general(a, b, (((1,), (1,)), ((), ())), preferred_element_type=jnp.float32)


def dot_tn(a, b):
    return lax.dot_general(a, b, (((0,), (0,)), ((), ())), preferred_element_type=jnp.float32)


def code_of(row, col):
    return (row + 16) * 64 + (col + 16)


def fine_code(s):
    return code_of(s >> 5, s & 31)


def patch_code(s):
    quarter, coarse = s >> 6, s & 63
    return code_of(2 * (coarse >> 4) + (quarter >> 1), 2 * (coarse & 15) + (quarter & 1))


def window_code(s):
    return code_of((s & 63) >> 3, 8 * (s >> 6) + (s & 7))


def rim_code(t):
    kind, c4 = t >> 5, t & 3
    row = jnp.where(kind < 2, (t & 31) >> 2, ((t & 15) >> 2) + jnp.where(kind == 2, 8, -4))
    west = jnp.where(kind < 2, kind & 1, (t >> 4) & 1)
    return code_of(row, c4 + 32 - 36 * west)


def iota(shape, axis):
    return lax.broadcasted_iota(jnp.int32, shape, axis)


def one_hot(same):
    return jnp.where(same, 1.0, 0.0).astype(jnp.bfloat16)


def fill_gather(ref, target_code, source_code, offset):
    target = target_code(iota((256, 128), 0)) + offset
    lane = iota((1, 128), 1)
    half = (lane >> 5 << 6) + (lane & 31)
    pieces = (
        source_code(lane),
        source_code(lane + 128),
        source_code(half + 32) - 8 * 64,
        source_code(half) + 8 * 64,
        rim_code(lane),
    )
    for n, piece in enumerate(pieces):
        ref[:, n * 128 : (n + 1) * 128] = one_hot(target == piece)


def fill_pack(ref, source_code):
    t = iota((64, 256), 0)
    target = code_of((t & 31) >> 2, (t & 3) + jnp.where(t >= 32, 28, 0))
    ref[...] = one_hot(target == source_code(iota((1, 256), 1)))


class Exchange:
    def __init__(self, where, source, pack, scratch):
        self.where, self.source, self.pack = where, source, pack
        self.packed, self.north, self.south, self.rim, self.ssem, self.rsem = scratch
        self.copies = []

    def make(self, n, source, target, lat, lon):
        return pltpu.make_async_remote_copy(
            src_ref=source,
            dst_ref=target,
            send_sem=self.ssem.at[n],
            recv_sem=self.rsem.at[n],
            device_id={
                "lat": lax.rem(self.where["lat"] + lat + 8, 8),
                "lon": lax.rem(self.where["lon"] + lon + 8, 8),
            },
            device_id_type=MESH,
        )

    def rows(self, quarter):
        first, last = pl.ds(0, 32), pl.ds(32, 32)
        return (
            self.make(quarter, self.source.at[quarter, :, first], self.south.at[quarter], -1, 0),
            self.make(quarter + 4, self.source.at[quarter, :, last], self.north.at[quarter], 1, 0),
        )

    def begin_rows(self, quarter):
        for made in self.rows(quarter):
            made.start()

    def begin_rim(self, quarters=(0, 1, 2, 3)):
        moves = jnp.concatenate([self.pack[:, q * 64 : (q + 1) * 64] for q in quarters], axis=1)
        for level in range(2):
            cells = jnp.concatenate([self.source[q, level] for q in quarters], axis=0)
            rim = dot(moves, cells).astype(jnp.bfloat16)
            self.packed[0, level] = rim[:32]
            self.packed[1, level] = rim[32:]
        near, far = pl.ds(0, 16), pl.ds(16, 16)
        packed, rim = self.packed, self.rim
        self.copies = [
            self.make(8, packed.at[0], rim.at[:, pl.ds(0, 32)], 0, -1),
            self.make(9, packed.at[1], rim.at[:, pl.ds(32, 32)], 0, 1),
            self.make(10, packed.at[0, :, near], rim.at[:, pl.ds(64, 16)], -1, -1),
            self.make(11, packed.at[1, :, near], rim.at[:, pl.ds(80, 16)], -1, 1),
            self.make(12, packed.at[0, :, far], rim.at[:, pl.ds(96, 16)], 1, -1),
            self.make(13, packed.at[1, :, far], rim.at[:, pl.ds(112, 16)], 1, 1),
        ]
        for made in self.copies:
            made.start()

    def begin(self):
        for quarter in range(4):
            self.begin_rows(quarter)
        self.begin_rim()

    def arrive(self):
        for quarter in range(4):
            self.copies += self.rows(quarter)
        for made in self.copies:
            made.wait_recv()

    def gather(self, level, moves):
        cells = jnp.concatenate(
            (
                self.source[:, level].reshape(256, 512),
                self.north[:, level].reshape(128, 512),
                self.south[:, level].reshape(128, 512),
                self.rim[level],
            ),
            axis=0,
        )
        return dot(moves[...], cells)

    def drain(self):
        for made in self.copies:
            made.wait_send()


def exchange_scratch():
    bf16 = jnp.bfloat16
    return [
        pltpu.VMEM((2, 2, 32, 512), bf16),
        pltpu.VMEM((4, 2, 32, 512), bf16),
        pltpu.VMEM((4, 2, 32, 512), bf16),
        pltpu.VMEM((2, 128, 512), bf16),
        pltpu.SemaphoreType.DMA((14,)),
        pltpu.SemaphoreType.DMA((14,)),
    ]


def send(source, target, ssem, rsem, device):
    made = pltpu.make_async_remote_copy(
        src_ref=source, dst_ref=target, send_sem=ssem, recv_sem=rsem, device_id=device, device_id_type=MESH
    )
    made.start()
    return made


def block_kernel(
    shifts_ref,
    bias_ref,
    fine_ref,
    cot_ref,
    land_ref,
    gain_attn_ref,
    gain_merge_ref,
    w_qkv_hbm,
    w_proj_hbm,
    w_merge_hbm,
    w_expand_hbm,
    out_ref,
    field_ref,
    qkv_out,
    proj_out,
    mg_out,
    ex_out,
    *scratch,
):
    scratch = list(scratch)

    def take(n):
        got = scratch[:n]
        del scratch[:n]
        return got

    f32, bf16 = jnp.float32, jnp.bfloat16
    w_qkv, w_proj, w_merge, w_expand, wsem = take(5)
    to_window, to_patch, pack_patch, pack_window = take(4)
    x_patch, c_patch, normed_w, hat_w, rstd_w = take(5)
    qkv, qkv_t, weights, branch = take(4)
    hidden, hat_m, rstd_m, merged, slope, act, gcoarse, out_patch, ghidden, gbranch = take(10)
    cots, gcoarses, act_t, merged_t, acts, mergeds, fsem, frsem = take(8)
    gbranch_w, gattended, gattended_t, gqkv, grolled, normed_t, attended_t = take(7)
    sib_normed, sib_attended, sib_gbranch, sib_gqkv, asem, arsem = take(6)
    acc_ex, acc_mg, acc_mh, acc_pj, acc_q1, acc_q2 = take(6)
    exchanges = [take(6) for _ in range(4)]
    streams_scratch = [take(6) for _ in range(6)]

    where = places()
    core, lat, lon = where["core"], where["lat"], where["lon"]
    loads = []
    for n, (far, near) in enumerate(
        ((w_qkv_hbm, w_qkv), (w_proj_hbm, w_proj), (w_merge_hbm, w_merge), (w_expand_hbm, w_expand))
    ):
        made = pltpu.make_async_copy(far, near, wsem.at[n])
        made.start()
        loads.append(made)

    barrier = pltpu.get_barrier_semaphore()
    beside = lon + 1 - 2 * where["z"]
    around = [(lat + a, lon + b) for a in (7, 8, 9) for b in (7, 8, 9) if (a, b) != (8, 8)]
    around += [(lat, lon + b) for b in range(2, 7)] + [(lat + a, lon) for a in (2, 4, 6)]
    around += [(lat + a, beside) for a in (2, 4, 6)]
    for a, b in around:
        pl.semaphore_signal(
            barrier, inc=1, device_id={"lat": lax.rem(a, 8), "lon": lax.rem(b, 8)}, device_id_type=MESH
        )

    shift_lat, shift_lon = shifts_ref[0], shifts_ref[1]
    low_lat = shift_lat <= 4
    off_lat = jnp.where(low_lat, shift_lat, shift_lat - 8)
    off_lon = jnp.where(shift_lon <= 4, shift_lon, shift_lon - 8)
    offset = off_lat * 64 + off_lon

    fill_pack(pack_patch, patch_code)
    arrange_hot = one_hot(patch_code(iota((256, 256), 0)) == fine_code(iota((1, 256), 1)))
    for source, target in ((fine_ref, x_patch), (cot_ref, c_patch)):
        for level in range(2):
            target[:, level] = dot(arrange_hot, source[level]).astype(bf16).reshape(4, 64, 512)
    pl.semaphore_wait(barrier, len(around))

    first = Exchange(where, x_patch, pack_patch, exchanges[0])
    first.begin()
    sent = []

    def share(n, source, target, name):
        made = send(source, target, fsem.at[n], frsem.at[n], where[name])
        sent.append(made)
        return made

    cot_side = share(0, c_patch, cots.at[0], "sibling")
    cot_beside = share(1, c_patch, cots.at[1], "beside")

    fill_gather(to_window, window_code, patch_code, offset)
    fill_gather(to_patch, patch_code, window_code, -offset)
    fill_pack(pack_window, window_code)

    (land_keys,) = take(1)

    def land_window(w, carry):
        key = iota((128, 256), 0)
        col_at = (32 * lon + off_lon + 8 * w + (key & 7) + 256) & 255
        land_rows = dot_nt(one_hot(iota((128, 256), 1) == col_at), land_ref[...].astype(bf16))
        row_at = (8 * lat + off_lat + ((iota((128, 64), 0) & 63) >> 3) + 64) & 63
        land = jnp.sum(jnp.where(iota((128, 64), 1) == row_at, land_rows, 0.0), axis=1, keepdims=True)
        land_keys[w] = jnp.broadcast_to(land, (128, 128))
        return carry

    lax.fori_loop(0, 4, land_window, 0)

    band = jnp.where(low_lat, lat, lax.rem(lat + 7, 8))

    def region(cell):
        row = 8 * band + ((cell & 63) >> 3)
        return jnp.where(row >= 56, 1, 0) + jnp.where(row >= 64 - shift_lat, 1, 0)

    same_region = region(iota((128, 128), 0)) == region(iota((128, 128), 1))
    heads = [jnp.where(iota((1, 128), 1) >> 5 == h, 1.0, 0.0).astype(bf16) for h in range(4)]

    def head_stack(value):
        return jnp.concatenate([value * head for head in heads], axis=0)

    def head_blocks(value):
        blocks = []
        for h in range(4):
            pieces = [value[32 * h : 32 * h + 32]]
            if h > 0:
                pieces.insert(0, jnp.zeros((32 * h, 128), bf16))
            if h < 3:
                pieces.append(jnp.zeros((96 - 32 * h, 128), bf16))
            blocks.append(jnp.concatenate(pieces, axis=0))
        return jnp.concatenate(blocks, axis=1)

    def under(value):
        return jnp.concatenate([value[:, h * 128 : (h + 1) * 128] for h in range(4)], axis=0)

    gain_attn = gain_attn_ref[...]
    first.arrive()
    for level in range(2):
        cells = first.gather(level, to_window)
        average = jnp.mean(cells, axis=-1, keepdims=True)
        centred = cells - average
        rstd = lax.rsqrt(jnp.mean(centred * centred, axis=-1, keepdims=True) + epsilon)
        hat = centred * rstd
        hat_w[:, level] = hat.reshape(4, 64, 512)
        rstd_w[:, level] = jnp.broadcast_to(rstd, (256, 128)).reshape(4, 64, 128)
        normed_w[:, level] = (hat * gain_attn).astype(bf16).reshape(4, 64, 512)

    loads[0].wait()
    normed = normed_w[...].reshape(512, 512)

    def project(n, carry):
        cols = w_qkv[:, pl.ds(pl.multiple_of(n * 256, 256), 256)]
        got = dot(normed_w[...].reshape(512, 512), cols).astype(bf16)
        for part in range(2):
            piece = got[:, part * 128 : (part + 1) * 128]
            qkv[2 * n + part] = piece.reshape(4, 128, 128)
            turned = piece.T
            for w in range(4):
                qkv_t[2 * n + part, w] = turned[:, w * 128 : (w + 1) * 128]
        return carry

    lax.fori_loop(0, 6, project, 0)
    normed_t[...] = normed.T.reshape(4, 2, 64, 512)
    pairs = [send(normed_t.at[:, 1 - core], sib_normed, asem.at[0], arsem.at[0], where["sibling"])]

    scale = 32.0 ** (-0.5)

    def attend(w, g):
        scores = dot(qkv[4 + g, w], head_blocks(qkv_t[g, w]))
        parts = []
        for h in range(4):
            score = scores[:, h * 128 : (h + 1) * 128] * scale + bias_ref[4 * g + h] * land_keys[w]
            score = jnp.where(same_region, score, -1000000000.0)
            raised = jnp.exp(score - jnp.max(score, axis=0, keepdims=True))
            parts.append((raised * (1.0 / jnp.sum(raised, axis=0, keepdims=True))).astype(bf16))
        weights[w, g] = jnp.concatenate(parts, axis=1)
        mixed = dot(head_blocks(qkv_t[8 + g, w]), jnp.concatenate(parts, axis=0))
        attended_t[g, :, :, pl.ds(pl.multiple_of(w * 128, 128), 128)] = mixed.astype(bf16).reshape(2, 64, 128)

    second = Exchange(where, branch, pack_window, exchanges[1])

    def attend_window(n, carry):
        w = lax.rem(3 * n, 4)
        for g in range(4):
            attend(w, g)
        mixed = attended_t[:, :, :, pl.ds(pl.multiple_of(w * 128, 128), 128)].reshape(512, 128).T
        branch[w] = dot(mixed, w_proj[...]).astype(bf16).reshape(2, 64, 512)
        second.begin_rows(w)
        return carry

    loads[1].wait()
    lax.fori_loop(0, 2, attend_window, 0)
    second.begin_rim((0, 3))
    lax.fori_loop(2, 4, attend_window, 0)
    pairs.append(send(attended_t.at[:, 1 - core], sib_attended, asem.at[1], arsem.at[1], where["sibling"]))
    second.arrive()
    for level in range(2):
        back = second.gather(level, to_patch).reshape(4, 64, 512)
        hidden[:, level] = (x_patch[:, level].astype(f32) + back.astype(bf16).astype(f32)).astype(bf16)

    def patches(ref):
        return jnp.concatenate([ref[q].reshape(128, 512) for q in range(4)], axis=1)

    gain_merge = gain_merge_ref[...]
    cells = patches(hidden).astype(f32)
    average = jnp.mean(cells, axis=-1, keepdims=True)
    centred = cells - average
    rstd = lax.rsqrt(jnp.mean(centred * centred, axis=-1, keepdims=True) + epsilon)
    hat = centred * rstd
    hat_m[...] = hat
    rstd_m[...] = jnp.broadcast_to(rstd, (128, 128))
    scaled = (hat * gain_merge).astype(bf16)
    for q in range(4):
        merged[q] = scaled[:, q * 512 : (q + 1) * 512]

    def part_rows(target, y, value):
        value = value.T.reshape(2, 4, 2, 16, 128)
        for c in range(2):
            for z in range(2):
                target[c, z, y] = value[c, :, z]

    for q in range(4):
        turned = scaled[:, q * 512 : (q + 1) * 512].T.reshape(2, 256, 128)
        for c in range(2):
            merged_t[c, q] = turned[c]
    side, level_z = 1 - core, where["z"]
    merged_side = share(3, merged_t.at[side], mergeds, "sibling")

    loads[2].wait()
    bend = 0.7978845608028654

    def merge(n, carry):
        rows = jnp.concatenate([merged[q] for q in range(4)], axis=1)
        coarse = dot(rows, w_merge[:, pl.ds(pl.multiple_of(n * 256, 256), 256)])
        square = coarse * coarse
        bent = jnp.tanh(bend * (coarse + 0.044715 * (coarse * square)))
        active = (0.5 * coarse * (1.0 + bent)).astype(bf16)
        act[n] = active
        part_rows(act_t, n, active)
        inner = bend * (1.0 + 3.0 * 0.044715 * square)
        slope[n] = 0.5 * (1.0 + bent) + 0.5 * coarse * (1.0 - bent * bent) * inner
        return carry

    lax.fori_loop(0, 4, merge, 0)
    act_parts = [
        share(6, act_t.at[side, level_z], acts.at[0], "sibling"),
        share(7, act_t.at[core, 1 - level_z], acts.at[1], "beside"),
        share(8, act_t.at[side, 1 - level_z], acts.at[2], "corner"),
    ]

    loads[3].wait()

    def back_expand(n, carry):
        rows = patches(c_patch)
        slab = w_expand[pl.ds(pl.multiple_of(n * 256, 256), 256), :]
        gcoarse[n] = (slope[n] * dot_nt(rows, slab)).astype(bf16)
        return carry

    lax.fori_loop(0, 4, back_expand, 0)
    gcoarse_side = share(9, gcoarse, gcoarses, "sibling")
    cot_beside.wait_recv()
    cot_corner = share(2, cots.at[1], cots.at[2], "sibling")

    def store_q1(value):
        qkv_out[:, 0:768] = value

    def store_q2(value):
        qkv_out[:, 768:1536] = value

    def store_pj(value):
        proj_out[...] = value

    def store_ex(value):
        ex_out[...] = value

    def store_mg(value):
        mg_out[:, 0:768] = value

    def store_mh(value):
        mg_out[:, 768:1024] = value

    stream_ex = Stream(where, acc_ex, "y", False, streams_scratch[0], store_ex)
    stream_mg = Stream(where, acc_mg, "x", True, streams_scratch[1], store_mg)
    stream_pj = Stream(where, acc_pj, "x", True, streams_scratch[2], store_pj)
    stream_q1 = Stream(where, acc_q1, "y", True, streams_scratch[3], store_q1)
    stream_q2 = Stream(where, acc_q2, "x", True, streams_scratch[4], store_q2)
    stream_mh = Stream(where, acc_mh, "y", True, streams_scratch[5], store_mh)
    def back_merge(q, carry):
        rows = jnp.concatenate([gcoarse[n] for n in range(4)], axis=1)
        slab = w_merge[pl.ds(pl.multiple_of(q * 512, 512), 512), :]
        ghidden[q] = dot_nt(rows, slab).reshape(2, 64, 512)
        return carry

    lax.fori_loop(0, 4, back_merge, 0)
    gain = [gain_merge[:, q * 512 : (q + 1) * 512] for q in range(4)]
    first_sum = jnp.zeros((128, 1), f32)
    second_sum = jnp.zeros((128, 1), f32)
    for q in range(4):
        grad = ghidden[q].reshape(128, 512) * gain[q]
        first_sum += jnp.sum(grad, axis=-1, keepdims=True)
        second_sum += jnp.sum(grad * hat_m[:, q * 512 : (q + 1) * 512], axis=-1, keepdims=True)
    first_sum, second_sum = first_sum / 2048.0, second_sum / 2048.0
    rstd = rstd_m[:, 0:1]
    for q in range(4):
        grad = ghidden[q].reshape(128, 512) * gain[q]
        grad = rstd * (grad - first_sum - hat_m[:, q * 512 : (q + 1) * 512] * second_sum)
        grad = grad + c_patch[q].reshape(128, 512).astype(f32)
        ghidden[q] = grad.reshape(2, 64, 512)
        gbranch[q] = grad.astype(bf16).reshape(2, 64, 512)

    third = Exchange(where, gbranch, pack_patch, exchanges[2])
    third.begin()

    merged_side.wait_recv()
    gcoarse_side.wait_recv()

    def merge_part(n):
        parts = [merged_t[core].reshape(1024, 128), mergeds[...].reshape(1024, 128)]
        left = jnp.concatenate(parts, axis=1)
        right = jnp.concatenate((gcoarse[n], gcoarses[n]), axis=0)
        return dot(left, right).astype(bf16).reshape(4, 4, 64, 256)

    def grad_merge(n, carry):
        acc_mg[:, :, :, pl.ds(pl.multiple_of(n * 256, 256), 256)] = merge_part(n)
        return carry

    lax.fori_loop(0, 3, grad_merge, 0)
    stream_mg.ring.begin()
    acc_mh[...] = merge_part(3)
    stream_mh.ring.begin()
    for made in act_parts:
        made.wait_recv()
    cot_side.wait_recv()
    cot_corner.wait_recv()

    def grad_expand(q, carry):
        parts = [act_t[core, level_z]] + [acts[n] for n in range(3)]
        left = jnp.concatenate([part.reshape(256, 128) for part in parts], axis=1)
        parts = [c_patch[q]] + [cots[n, q] for n in range(3)]
        right = jnp.concatenate([part.reshape(128, 512) for part in parts], axis=0)
        got = dot(left, right).astype(bf16).reshape(4, 4, 16, 512)
        acc_ex[:, :, :, pl.ds(pl.multiple_of(q * 512, 512), 512)] = got
        return carry

    lax.fori_loop(0, 4, grad_expand, 0)
    stream_ex.ring.begin()

    third.arrive()
    for level in range(2):
        gbranch_w[:, level] = third.gather(level, to_window).astype(bf16).reshape(4, 64, 512)
    grads_w = gbranch_w[...].reshape(512, 512)
    gattended[...] = dot_nt(grads_w, w_proj[...]).astype(bf16).reshape(4, 128, 512)
    turned = dot_nt(w_proj[...], grads_w).astype(bf16)
    for w in range(4):
        gattended_t[w] = turned[:, w * 128 : (w + 1) * 128].reshape(4, 128, 128)
    pairs.append(send(gbranch_w, sib_gbranch, asem.at[2], arsem.at[2], where["sibling"]))

    def share_window(w):
        return pltpu.make_async_remote_copy(
            src_ref=gqkv.at[:, w],
            dst_ref=sib_gqkv.at[:, w],
            send_sem=asem.at[3 + w],
            recv_sem=arsem.at[3 + w],
            device_id=where["sibling"],
            device_id_type=MESH,
        )

    def attend_back(w, g):
        grads = gattended[w, :, g * 128 : (g + 1) * 128]
        grad_weights = dot(qkv[8 + g, w], head_blocks(gattended_t[w, g]))
        weight = weights[w, g]
        wide = weight.astype(f32)
        shared = wide * grad_weights
        delta = jnp.sum(shared, axis=0, keepdims=True)
        grad_scores = ((shared - wide * delta) * scale).astype(bf16)
        turned = dot(head_blocks(qkv_t[4 + g, w]), under(grad_scores))
        gqkv[g, w] = turned.astype(bf16).T
        gqkv[4 + g, w] = dot(grad_scores, head_stack(qkv[g, w])).astype(bf16)
        gqkv[8 + g, w] = dot(weight, head_stack(grads)).astype(bf16)

    def attend_back_window(w, carry):
        for g in range(4):
            attend_back(w, g)
        share_window(w).start()
        return carry

    lax.fori_loop(0, 2, attend_back_window, 0)
    for made in pairs:
        made.wait_recv()
    left = jnp.concatenate((attended_t[:, core].reshape(256, 512), sib_attended[...].reshape(256, 512)), axis=1)
    right = jnp.concatenate((gbranch_w[...].reshape(512, 512), sib_gbranch[...].reshape(512, 512)), axis=0)
    acc_pj[...] = dot(left, right).astype(bf16).reshape(4, 4, 16, 512)
    stream_pj.ring.begin()
    stream_ex.ring.middle()
    stream_mg.ring.middle()
    stream_mh.ring.middle()
    lax.fori_loop(2, 4, attend_back_window, 0)
    windows = [share_window(w) for w in range(4)]
    for made in windows:
        made.wait_recv()

    def grad_qkv(target, base, n, carry):
        left = jnp.concatenate((normed_t[:, core].reshape(256, 512), sib_normed[...].reshape(256, 512)), axis=1)
        k = 2 * n + base
        own = [gqkv[k + part].reshape(512, 128) for part in range(2)]
        far = [sib_gqkv[k + part].reshape(512, 128) for part in range(2)]
        right = jnp.concatenate((jnp.concatenate(own, axis=1), jnp.concatenate(far, axis=1)), axis=0)
        got = dot(left, right).astype(bf16).reshape(4, 4, 16, 256)
        target[:, :, :, pl.ds(pl.multiple_of(n * 256, 256), 256)] = got
        return carry

    lax.fori_loop(0, 3, functools.partial(grad_qkv, acc_q1, 0), 0)
    stream_q1.ring.begin()
    lax.fori_loop(0, 3, functools.partial(grad_qkv, acc_q2, 6), 0)
    stream_q2.ring.begin()
    stream_ex.ring.finish()
    stream_ex.spread()

    def norm_back(half, carry):
        rows = jnp.concatenate([gqkv[n, pl.ds(2 * half, 2)].reshape(256, 128) for n in range(12)], axis=1)
        grad = dot_nt(rows, w_qkv[...]) * gain_attn
        hat = hat_w[pl.ds(2 * half, 2)].reshape(256, 512)
        rstd = rstd_w[pl.ds(2 * half, 2)].reshape(256, 128)[:, 0:1]
        first_mean = jnp.mean(grad, axis=-1, keepdims=True)
        second_mean = jnp.mean(grad * hat, axis=-1, keepdims=True)
        grad = rstd * (grad - first_mean - hat * second_mean)
        grolled[pl.ds(2 * half, 2)] = grad.astype(bf16).reshape(2, 2, 64, 512)
        return carry

    lax.fori_loop(0, 2, norm_back, 0)
    fourth = Exchange(where, grolled, pack_window, exchanges[3])
    fourth.begin()
    stream_mh.ring.finish()
    stream_mh.spread()
    stream_mg.ring.finish()
    stream_mg.spread()
    stream_pj.ring.middle()
    stream_q1.ring.middle()
    stream_q2.ring.middle()

    fine_hot = one_hot(fine_code(iota((256, 256), 0)) == patch_code(iota((1, 256), 1)))

    def expand(q, carry):
        rows = jnp.concatenate([act[n] for n in range(4)], axis=1)
        grown = dot(rows, w_expand[:, pl.ds(pl.multiple_of(q * 512, 512), 512)])
        out_patch[q] = (hidden[q].reshape(128, 512).astype(f32) + grown).astype(bf16).reshape(2, 64, 512)
        return carry

    lax.fori_loop(0, 4, expand, 0)
    for level in range(2):
        out_ref[level] = dot(fine_hot, out_patch[:, level].reshape(256, 512)).astype(bf16)

    stream_pj.ring.finish()
    stream_pj.spread()
    stream_q1.ring.finish()
    stream_q1.spread()
    stream_q2.ring.finish()
    stream_q2.spread()
    fourth.arrive()
    for level in range(2):
        back = fourth.gather(level, to_patch).astype(bf16).astype(f32)
        total = (ghidden[:, level].reshape(256, 512) + back).astype(bf16)
        field_ref[level] = dot(fine_hot, total).astype(bf16)

    streams = (stream_ex, stream_mh, stream_mg, stream_pj, stream_q1, stream_q2)
    for stream in streams:
        stream.end()

    for made in sent + pairs + windows:
        made.wait_send()
    for each in (first, second, third, fourth):
        each.drain()
    for stream in streams:
        stream.drain()


def deliver_kernel(*refs):
    sources, targets, held, sems = refs[:6], refs[6:12], refs[12:18], refs[18]
    loads = [pltpu.make_async_copy(a, b, sems.at[0, n]) for n, (a, b) in enumerate(zip(sources, held))]
    stores = [pltpu.make_async_copy(a, b, sems.at[1, n]) for n, (a, b) in enumerate(zip(held, targets))]
    for made in loads:
        made.start()
    for load, store in zip(loads, stores):
        load.wait()
        store.start()
    for made in stores:
        made.wait()


def deliver(results):
    hbm = pl.BlockSpec(memory_space=pl.ANY)
    return pl.pallas_call(
        deliver_kernel,
        out_shape=tuple(jax.ShapeDtypeStruct(r.shape, r.dtype) for r in results),
        in_specs=[hbm] * 6,
        out_specs=(hbm,) * 6,
        scratch_shapes=[pltpu.VMEM(r.shape, r.dtype) for r in results] + [pltpu.SemaphoreType.DMA((2, 6))],
        name="deliver",
    )(*results)


def on_device(
    fine_field,
    cotangent,
    land_sea,
    shifts,
    gain_attn,
    w_qkv,
    w_proj,
    land_bias,
    gain_merge,
    w_merge,
    w_expand,
):
    vmem = pl.BlockSpec(memory_space=pltpu.VMEM)
    smem = pl.BlockSpec(memory_space=pltpu.SMEM)
    hbm = pl.BlockSpec(memory_space=pl.ANY)
    f32, bf16 = jnp.float32, jnp.bfloat16
    cells = (4, 2, 64, 512)
    scratch = [
        pltpu.VMEM((512, 1536), bf16),
        pltpu.VMEM((512, 512), bf16),
        pltpu.VMEM((2048, 1024), bf16),
        pltpu.VMEM((1024, 2048), bf16),
        pltpu.SemaphoreType.DMA((4,)),
        pltpu.VMEM((256, 640), bf16),
        pltpu.VMEM((256, 640), bf16),
        pltpu.VMEM((64, 256), bf16),
        pltpu.VMEM((64, 256), bf16),
        pltpu.VMEM(cells, bf16),
        pltpu.VMEM(cells, bf16),
        pltpu.VMEM(cells, bf16),
        pltpu.VMEM(cells, f32),
        pltpu.VMEM((4, 2, 64, 128), f32),
        pltpu.VMEM((12, 4, 128, 128), bf16),
        pltpu.VMEM((12, 4, 128, 128), bf16),
        pltpu.VMEM((4, 4, 128, 512), bf16),
        pltpu.VMEM(cells, bf16),
        pltpu.VMEM(cells, bf16),
        pltpu.VMEM((128, 2048), f32),
        pltpu.VMEM((128, 128), f32),
        pltpu.VMEM((4, 128, 512), bf16),
        pltpu.VMEM((4, 128, 256), f32),
        pltpu.VMEM((4, 128, 256), bf16),
        pltpu.VMEM((4, 128, 256), bf16),
        pltpu.VMEM(cells, bf16),
        pltpu.VMEM(cells, f32),
        pltpu.VMEM(cells, bf16),
        pltpu.VMEM((3,) + cells, bf16),
        pltpu.VMEM((4, 128, 256), bf16),
        pltpu.VMEM((2, 2, 4, 4, 16, 128), bf16),
        pltpu.VMEM((2, 4, 256, 128), bf16),
        pltpu.VMEM((3, 4, 4, 16, 128), bf16),
        pltpu.VMEM((4, 256, 128), bf16),
        pltpu.SemaphoreType.DMA((12,)),
        pltpu.SemaphoreType.DMA((12,)),
        pltpu.VMEM(cells, bf16),
        pltpu.VMEM((4, 128, 512), bf16),
        pltpu.VMEM((4, 4, 128, 128), bf16),
        pltpu.VMEM((12, 4, 128, 128), bf16),
        pltpu.VMEM(cells, bf16),
        pltpu.VMEM(cells, bf16),
        pltpu.VMEM(cells, bf16),
        pltpu.VMEM((4, 64, 512), bf16),
        pltpu.VMEM((4, 64, 512), bf16),
        pltpu.VMEM(cells, bf16),
        pltpu.VMEM((12, 4, 128, 128), bf16),
        pltpu.SemaphoreType.DMA((7,)),
        pltpu.SemaphoreType.DMA((7,)),
        pltpu.VMEM((4, 4, 16, 2048), bf16),
        pltpu.VMEM((4, 4, 64, 768), bf16),
        pltpu.VMEM((4, 4, 64, 256), bf16),
        pltpu.VMEM((4, 4, 16, 512), bf16),
        pltpu.VMEM((4, 4, 16, 768), bf16),
        pltpu.VMEM((4, 4, 16, 768), bf16),
    ]
    for _ in range(4):
        scratch += exchange_scratch()
    scratch += stream_scratch(16, 2048, False)
    scratch += stream_scratch(64, 768, True)
    scratch += stream_scratch(16, 512, True)
    scratch += stream_scratch(16, 768, True)
    scratch += stream_scratch(16, 768, True)
    scratch += stream_scratch(64, 256, True)
    scratch += [pltpu.VMEM((4, 128, 128), f32)]
    results = pl.pallas_call(
        block_kernel,
        out_shape=(
            jax.ShapeDtypeStruct((2, 256, 512), bf16),
            jax.ShapeDtypeStruct((2, 256, 512), bf16),
            jax.ShapeDtypeStruct((8, 1536), f32),
            jax.ShapeDtypeStruct((8, 512), f32),
            jax.ShapeDtypeStruct((32, 1024), f32),
            jax.ShapeDtypeStruct((16, 2048), f32),
        ),
        in_specs=[smem, smem] + [vmem] * 5 + [hbm] * 4,
        out_specs=(vmem,) * 6,
        scratch_shapes=scratch,
        compiler_params=pltpu.CompilerParams(
            collective_id=0, has_side_effects=True, vmem_limit_bytes=60 * 2**20
        ),
        name="attention_block",
    )(
        shifts,
        land_bias,
        fine_field.reshape(2, 256, 512),
        cotangent.reshape(2, 256, 512),
        land_sea,
        gain_attn.reshape(1, 512),
        gain_merge.reshape(1, 2048),
        w_qkv,
        w_proj,
        w_merge,
        w_expand,
    )
    results = deliver(results)
    output, grad_field = results[0].reshape(2, 8, 32, 512), results[1].reshape(2, 8, 32, 512)
    return (output, grad_field) + tuple(results[2:])


def solution(mesh):
    return jax.shard_map(
        on_device,
        mesh=mesh,
        in_specs=(
            P("rep", "lat", "lon", None),
            P("rep", "lat", "lon", None),
            P(),
            P(),
            P(),
            P(),
            P(),
            P(),
            P(),
            P(),
            P(),
        ),
        out_specs=(
            P("rep", "lat", "lon", None),
            P("rep", "lat", "lon", None),
            P(("rep", "lat", "lon"), None),
            P(("rep", "lat", "lon"), None),
            P(("rep", "lat", "lon"), None),
            P(("rep", "lat", "lon"), None),
        ),
        check_vma=False,
    )
```

```python
import functools

import jax
import jax.numpy as jnp
from jax import lax
from jax.experimental import pallas as pl
from jax.experimental.pallas import tpu as pltpu
from jax.sharding import PartitionSpec as P

epsilon = 1e-05

MESH = pl.DeviceIdType.MESH


class Ring:
    def __init__(self, place, right, left, block, store, bufs, send_sems, recv_sems, half):
        self.place, self.right, self.left = place, right, left
        self.block, self.store = block, store
        self.bufs, self.outs = bufs[0], bufs[1]
        self.send_sems, self.recv_sems = send_sems, recv_sems
        self.half = half
        self.copies = {}

    def part(self, k, which):
        return self.block(k).at[:, :, pl.ds(which * self.half, self.half)]

    def copy(self, slot, source, target):
        made = pltpu.make_async_remote_copy(
            src_ref=source,
            dst_ref=self.bufs.at[slot],
            send_sem=self.send_sems.at[slot],
            recv_sem=self.recv_sems.at[slot],
            device_id=target,
            device_id_type=MESH,
        )
        made.start()
        self.copies[slot] = made

    def begin(self):
        ahead = lax.rem(self.place + 1, 4)
        across = lax.rem(self.place + 2, 4)
        behind = lax.rem(self.place + 3, 4)
        self.copy(0, self.part(across, 0), self.right)
        self.copy(3, self.part(across, 1), self.left)
        self.copy(1, self.part(ahead, 1), self.right)
        self.copy(4, self.part(behind, 0), self.left)

    def middle(self):
        ahead = lax.rem(self.place + 1, 4)
        behind = lax.rem(self.place + 3, 4)
        for slot, which, k, out, target in ((0, 0, ahead, 0, self.right), (3, 1, behind, 1, self.left)):
            self.copies[slot].wait_recv()

            def add(i, carry, slot=slot, which=which, k=k, out=out):
                mine = self.block(k)[i, :, pl.ds(which * self.half, self.half)]
                total = mine.astype(jnp.float32) + self.bufs[slot, i].astype(jnp.float32)
                self.outs[out, i] = total.astype(jnp.bfloat16)
                return carry

            lax.fori_loop(0, 4, add, 0)
            self.copy(2 if out == 0 else 5, self.outs.at[out], target)

    def finish(self):
        for slot in (1, 2, 4, 5):
            self.copies[slot].wait_recv()

        def add(i, carry):
            totals = []
            for which, first, second in ((0, 2, 4), (1, 5, 1)):
                mine = self.block(self.place)[i, :, pl.ds(which * self.half, self.half)]
                totals.append(
                    mine.astype(jnp.float32)
                    + self.bufs[first, i].astype(jnp.float32)
                    + self.bufs[second, i].astype(jnp.float32)
                )
            self.store(i, totals[0], totals[1])
            return carry

        lax.fori_loop(0, 4, add, 0)

    def drain(self):
        for slot in range(6):
            self.copies[slot].wait_send()


class Stream:
    def __init__(self, where, source, first_axis, paired, scratch, store):
        buf, out, red, got, ssem, rsem = scratch
        self.where, self.paired, self.store = where, paired, store
        self.red, self.got, self.ssem, self.rsem = red, got, ssem, rsem
        self.half, self.deep = source.shape[3] // 2, source.shape[2] // 2
        axes = {
            "y": (where["y"], where["up"], where["down"], lambda k: source.at[k]),
            "x": (where["x"], where["east"], where["west"], lambda k: source.at[:, k]),
        }
        self.second_axis = "x" if first_axis == "y" else "y"
        place, right, left, block = axes[first_axis]
        self.ring = Ring(place, right, left, block, self.keep, (buf, out), ssem, rsem, self.half)
        self.place = where[self.second_axis]

    def keep(self, i, first, second):
        if self.paired:
            for z in range(2):
                rows = slice(z * self.deep, (z + 1) * self.deep)
                both = jnp.concatenate((first[rows], second[rows]), axis=0 if self.deep == 8 else 1)
                self.red[i, z] = both.astype(jnp.bfloat16)
        else:
            self.red[i] = jnp.concatenate((first, second), axis=1).astype(jnp.bfloat16)

    def spread(self):
        where = self.where
        self.copies = []
        for n in range(1, 8 if self.paired else 4):
            d, e = (n // 2, n % 2) if self.paired else (n, 0)
            k = lax.rem(self.place + d, 4)
            block = self.red.at[k, where["z"] * (1 - e) + (1 - where["z"]) * e] if self.paired else self.red.at[k]
            if self.second_axis == "x":
                lon = lax.rem(where["lon"] + 2 * d, 8)
                target = {"lon": lon + e * (1 - 2 * where["z"])}
            else:
                target = {
                    "lat": lax.rem(where["lat"] + 2 * d, 8),
                    "lon": where["lon"] + e * (1 - 2 * where["z"]),
                }
            made = pltpu.make_async_remote_copy(
                src_ref=block,
                dst_ref=self.got.at[n - 1],
                send_sem=self.ssem.at[5 + n],
                recv_sem=self.rsem.at[5 + n],
                device_id=target,
                device_id_type=MESH,
            )
            made.start()
            self.copies.append(made)

    def end(self):
        for made in self.copies:
            made.wait_recv()
        mine = self.red[self.place, self.where["z"]] if self.paired else self.red[self.place]
        total = mine.astype(jnp.float32)
        for n in range(len(self.copies)):
            total += self.got[n].astype(jnp.float32)
        if self.paired and self.deep == 8:
            total = jnp.concatenate((total[:8], total[8:]), axis=1)
        self.store(total)

    def drain(self):
        self.ring.drain()
        for made in self.copies:
            made.wait_send()


def stream_scratch(rows, width, paired):
    half, bf16 = width // 2, jnp.bfloat16
    block = (16, half) if rows == 16 else (rows // 2, width)
    return [
        pltpu.VMEM((6, 4, rows, half), bf16),
        pltpu.VMEM((2, 4, rows, half), bf16),
        pltpu.VMEM((4, 2) + block if paired else (4, rows, width), bf16),
        pltpu.VMEM((7,) + block if paired else (3, rows, width), bf16),
        pltpu.SemaphoreType.DMA((13,)),
        pltpu.SemaphoreType.DMA((13,)),
    ]


def places():
    lat, lon = lax.axis_index("lat"), lax.axis_index("lon")
    core, z = lax.rem(lat, 2), lax.rem(lon, 2)
    return {
        "lat": lat,
        "lon": lon,
        "y": lat // 2,
        "x": lon // 2,
        "core": core,
        "z": z,
        "up": {"lat": lax.rem(lat + 2, 8)},
        "down": {"lat": lax.rem(lat + 6, 8)},
        "east": {"lon": lax.rem(lon + 2, 8)},
        "west": {"lon": lax.rem(lon + 6, 8)},
        "beside": {"lon": lon + 1 - 2 * z},
        "sibling": {"lat": lat + 1 - 2 * core},
        "corner": {"lat": lat + 1 - 2 * core, "lon": lon + 1 - 2 * z},
    }


def dot(a, b):
    return lax.dot_general(a, b, (((1,), (0,)), ((), ())), preferred_element_type=jnp.float32)


def dot_nt(a, b):
    return lax.dot_general(a, b, (((1,), (1,)), ((), ())), preferred_element_type=jnp.float32)


def dot_tn(a, b):
    return lax.dot_general(a, b, (((0,), (0,)), ((), ())), preferred_element_type=jnp.float32)


def code_of(row, col):
    return (row + 16) * 64 + (col + 16)


def fine_code(s):
    return code_of(s >> 5, s & 31)


def patch_code(s):
    quarter, coarse = s >> 6, s & 63
    return code_of(2 * (coarse >> 4) + (quarter >> 1), 2 * (coarse & 15) + (quarter & 1))


def window_code(s):
    return code_of((s & 63) >> 3, 8 * (s >> 6) + (s & 7))


def rim_code(t):
    kind, c4 = t >> 5, t & 3
    row = jnp.where(kind < 2, (t & 31) >> 2, ((t & 15) >> 2) + jnp.where(kind == 2, 8, -4))
    west = jnp.where(kind < 2, kind & 1, (t >> 4) & 1)
    return code_of(row, c4 + 32 - 36 * west)


def iota(shape, axis):
    return lax.broadcasted_iota(jnp.int32, shape, axis)


def one_hot(same):
    return jnp.where(same, 1.0, 0.0).astype(jnp.bfloat16)


def fill_gather(ref, target_code, source_code, offset):
    target = target_code(iota((256, 128), 0)) + offset
    lane = iota((1, 128), 1)
    half = (lane >> 5 << 6) + (lane & 31)
    pieces = (
        source_code(lane),
        source_code(lane + 128),
        source_code(half + 32) - 8 * 64,
        source_code(half) + 8 * 64,
        rim_code(lane),
    )
    for n, piece in enumerate(pieces):
        ref[:, n * 128 : (n + 1) * 128] = one_hot(target == piece)


def fill_pack(ref, source_code):
    t = iota((64, 256), 0)
    target = code_of((t & 31) >> 2, (t & 3) + jnp.where(t >= 32, 28, 0))
    ref[...] = one_hot(target == source_code(iota((1, 256), 1)))


class Exchange:
    def __init__(self, where, source, pack, scratch):
        self.where, self.source, self.pack = where, source, pack
        self.packed, self.north, self.south, self.rim, self.ssem, self.rsem = scratch
        self.copies = []

    def make(self, n, source, target, lat, lon):
        return pltpu.make_async_remote_copy(
            src_ref=source,
            dst_ref=target,
            send_sem=self.ssem.at[n],
            recv_sem=self.rsem.at[n],
            device_id={
                "lat": lax.rem(self.where["lat"] + lat + 8, 8),
                "lon": lax.rem(self.where["lon"] + lon + 8, 8),
            },
            device_id_type=MESH,
        )

    def rows(self, quarter):
        first, last = pl.ds(0, 32), pl.ds(32, 32)
        return (
            self.make(quarter, self.source.at[quarter, :, first], self.south.at[quarter], -1, 0),
            self.make(quarter + 4, self.source.at[quarter, :, last], self.north.at[quarter], 1, 0),
        )

    def begin_rows(self, quarter):
        for made in self.rows(quarter):
            made.start()

    def begin_rim(self, quarters=(0, 1, 2, 3)):
        moves = jnp.concatenate([self.pack[:, q * 64 : (q + 1) * 64] for q in quarters], axis=1)
        for level in range(2):
            cells = jnp.concatenate([self.source[q, level] for q in quarters], axis=0)
            rim = dot(moves, cells).astype(jnp.bfloat16)
            self.packed[0, level] = rim[:32]
            self.packed[1, level] = rim[32:]
        near, far = pl.ds(0, 16), pl.ds(16, 16)
        packed, rim = self.packed, self.rim
        self.copies = [
            self.make(8, packed.at[0], rim.at[:, pl.ds(0, 32)], 0, -1),
            self.make(9, packed.at[1], rim.at[:, pl.ds(32, 32)], 0, 1),
            self.make(10, packed.at[0, :, near], rim.at[:, pl.ds(64, 16)], -1, -1),
            self.make(11, packed.at[1, :, near], rim.at[:, pl.ds(80, 16)], -1, 1),
            self.make(12, packed.at[0, :, far], rim.at[:, pl.ds(96, 16)], 1, -1),
            self.make(13, packed.at[1, :, far], rim.at[:, pl.ds(112, 16)], 1, 1),
        ]
        for made in self.copies:
            made.start()

    def begin(self):
        for quarter in range(4):
            self.begin_rows(quarter)
        self.begin_rim()

    def arrive(self):
        for quarter in range(4):
            self.copies += self.rows(quarter)
        for made in self.copies:
            made.wait_recv()

    def gather(self, level, moves):
        cells = jnp.concatenate(
            (
                self.source[:, level].reshape(256, 512),
                self.north[:, level].reshape(128, 512),
                self.south[:, level].reshape(128, 512),
                self.rim[level],
            ),
            axis=0,
        )
        return dot(moves[...], cells)

    def drain(self):
        for made in self.copies:
            made.wait_send()


def exchange_scratch():
    bf16 = jnp.bfloat16
    return [
        pltpu.VMEM((2, 2, 32, 512), bf16),
        pltpu.VMEM((4, 2, 32, 512), bf16),
        pltpu.VMEM((4, 2, 32, 512), bf16),
        pltpu.VMEM((2, 128, 512), bf16),
        pltpu.SemaphoreType.DMA((14,)),
        pltpu.SemaphoreType.DMA((14,)),
    ]


def send(source, target, ssem, rsem, device):
    made = pltpu.make_async_remote_copy(
        src_ref=source, dst_ref=target, send_sem=ssem, recv_sem=rsem, device_id=device, device_id_type=MESH
    )
    made.start()
    return made


def block_kernel(
    shifts_ref,
    bias_ref,
    fine_ref,
    cot_hbm,
    land_ref,
    gain_attn_ref,
    gain_merge_ref,
    w_qkv_hbm,
    w_proj_hbm,
    w_merge_hbm,
    w_expand_hbm,
    out_hbm,
    field_hbm,
    qkv_out,
    proj_out,
    mg_out,
    ex_out,
    *scratch,
):
    scratch = list(scratch)

    def take(n):
        got = scratch[:n]
        del scratch[:n]
        return got

    f32, bf16 = jnp.float32, jnp.bfloat16
    w_qkv, w_proj, w_merge, w_expand, cot_ref, out_ref, field_ref, wsem = take(8)
    cot_load = pltpu.make_async_copy(cot_hbm, cot_ref, wsem.at[4])
    cot_load.start()
    to_window, to_patch, pack_patch, pack_window = take(4)
    x_patch, c_patch, normed_w, hat_w, rstd_w = take(5)
    qkv, qkv_t, weights, branch = take(4)
    hidden, hat_m, rstd_m, merged, slope, act, gcoarse, out_patch, ghidden, gbranch = take(10)
    cots, gcoarses, act_t, merged_t, acts, mergeds, fsem, frsem = take(8)
    gbranch_w, gattended, gattended_t, gqkv, grolled, normed_t, attended_t = take(7)
    sib_normed, sib_attended, sib_gbranch, sib_gqkv, asem, arsem = take(6)
    acc_ex, acc_mg, acc_mh, acc_pj, acc_q1, acc_q2 = take(6)
    exchanges = [take(6) for _ in range(4)]
    streams_scratch = [take(6) for _ in range(6)]

    where = places()
    core, lat, lon = where["core"], where["lat"], where["lon"]
    loads = []
    for n, (far, near) in enumerate(
        ((w_qkv_hbm, w_qkv), (w_proj_hbm, w_proj), (w_merge_hbm, w_merge), (w_expand_hbm, w_expand))
    ):
        made = pltpu.make_async_copy(far, near, wsem.at[n])
        made.start()
        loads.append(made)

    barrier = pltpu.get_barrier_semaphore()
    beside = lon + 1 - 2 * where["z"]
    around = [(lat + a, lon + b) for a in (7, 8, 9) for b in (7, 8, 9) if (a, b) != (8, 8)]
    around += [(lat, lon + b) for b in range(2, 7)] + [(lat + a, lon) for a in (2, 4, 6)]
    around += [(lat + a, beside) for a in (2, 4, 6)]
    for a, b in around:
        pl.semaphore_signal(
            barrier, inc=1, device_id={"lat": lax.rem(a, 8), "lon": lax.rem(b, 8)}, device_id_type=MESH
        )

    shift_lat, shift_lon = shifts_ref[0], shifts_ref[1]
    low_lat = shift_lat <= 4
    off_lat = jnp.where(low_lat, shift_lat, shift_lat - 8)
    off_lon = jnp.where(shift_lon <= 4, shift_lon, shift_lon - 8)
    offset = off_lat * 64 + off_lon

    fill_pack(pack_patch, patch_code)
    arrange_hot = one_hot(patch_code(iota((256, 256), 0)) == fine_code(iota((1, 256), 1)))
    for level in range(2):
        x_patch[:, level] = dot(arrange_hot, fine_ref[level]).astype(bf16).reshape(4, 64, 512)
    pl.semaphore_wait(barrier, len(around))

    first = Exchange(where, x_patch, pack_patch, exchanges[0])
    first.begin()
    cot_load.wait()
    for level in range(2):
        c_patch[:, level] = dot(arrange_hot, cot_ref[level]).astype(bf16).reshape(4, 64, 512)
    sent = []

    def share(n, source, target, name):
        made = send(source, target, fsem.at[n], frsem.at[n], where[name])
        sent.append(made)
        return made

    cot_side = share(0, c_patch, cots.at[0], "sibling")
    cot_beside = share(1, c_patch, cots.at[1], "beside")

    fill_gather(to_window, window_code, patch_code, offset)
    fill_gather(to_patch, patch_code, window_code, -offset)
    fill_pack(pack_window, window_code)

    (land_keys,) = take(1)

    def land_window(w, carry):
        key = iota((128, 256), 0)
        col_at = (32 * lon + off_lon + 8 * w + (key & 7) + 256) & 255
        land_rows = dot_nt(one_hot(iota((128, 256), 1) == col_at), land_ref[...].astype(bf16))
        row_at = (8 * lat + off_lat + ((iota((128, 64), 0) & 63) >> 3) + 64) & 63
        land = jnp.sum(jnp.where(iota((128, 64), 1) == row_at, land_rows, 0.0), axis=1, keepdims=True)
        land_keys[w] = jnp.broadcast_to(land, (128, 128))
        return carry

    lax.fori_loop(0, 4, land_window, 0)

    band = jnp.where(low_lat, lat, lax.rem(lat + 7, 8))

    def region(cell):
        row = 8 * band + ((cell & 63) >> 3)
        return jnp.where(row >= 56, 1, 0) + jnp.where(row >= 64 - shift_lat, 1, 0)

    same_region = region(iota((128, 128), 0)) == region(iota((128, 128), 1))
    heads = [jnp.where(iota((1, 128), 1) >> 5 == h, 1.0, 0.0).astype(bf16) for h in range(4)]

    def head_stack(value):
        return jnp.concatenate([value * head for head in heads], axis=0)

    def head_blocks(value):
        blocks = []
        for h in range(4):
            pieces = [value[32 * h : 32 * h + 32]]
            if h > 0:
                pieces.insert(0, jnp.zeros((32 * h, 128), bf16))
            if h < 3:
                pieces.append(jnp.zeros((96 - 32 * h, 128), bf16))
            blocks.append(jnp.concatenate(pieces, axis=0))
        return jnp.concatenate(blocks, axis=1)

    def under(value):
        return jnp.concatenate([value[:, h * 128 : (h + 1) * 128] for h in range(4)], axis=0)

    gain_attn = gain_attn_ref[...]
    first.arrive()
    for level in range(2):
        cells = first.gather(level, to_window)
        average = jnp.mean(cells, axis=-1, keepdims=True)
        centred = cells - average
        rstd = lax.rsqrt(jnp.mean(centred * centred, axis=-1, keepdims=True) + epsilon)
        hat = centred * rstd
        hat_w[:, level] = hat.reshape(4, 64, 512)
        rstd_w[:, level] = jnp.broadcast_to(rstd, (256, 128)).reshape(4, 64, 128)
        normed_w[:, level] = (hat * gain_attn).astype(bf16).reshape(4, 64, 512)

    loads[0].wait()
    normed = normed_w[...].reshape(512, 512)

    def project(n, carry):
        cols = w_qkv[:, pl.ds(pl.multiple_of(n * 256, 256), 256)]
        got = dot(normed_w[...].reshape(512, 512), cols).astype(bf16)
        for part in range(2):
            piece = got[:, part * 128 : (part + 1) * 128]
            qkv[2 * n + part] = piece.reshape(4, 128, 128)
            turned = piece.T
            for w in range(4):
                qkv_t[2 * n + part, w] = turned[:, w * 128 : (w + 1) * 128]
        return carry

    lax.fori_loop(0, 6, project, 0)
    normed_t[...] = normed.T.reshape(4, 2, 64, 512)
    pairs = [send(normed_t.at[:, 1 - core], sib_normed, asem.at[0], arsem.at[0], where["sibling"])]

    scale = 32.0 ** (-0.5)

    def attend(w, g):
        scores = dot(qkv[4 + g, w], head_blocks(qkv_t[g, w]))
        parts = []
        for h in range(4):
            score = scores[:, h * 128 : (h + 1) * 128] * scale + bias_ref[4 * g + h] * land_keys[w]
            score = jnp.where(same_region, score, -1000000000.0)
            raised = jnp.exp(score - jnp.max(score, axis=0, keepdims=True))
            parts.append((raised * (1.0 / jnp.sum(raised, axis=0, keepdims=True))).astype(bf16))
        weights[w, g] = jnp.concatenate(parts, axis=1)
        mixed = dot(head_blocks(qkv_t[8 + g, w]), jnp.concatenate(parts, axis=0))
        attended_t[g, :, :, pl.ds(pl.multiple_of(w * 128, 128), 128)] = mixed.astype(bf16).reshape(2, 64, 128)

    second = Exchange(where, branch, pack_window, exchanges[1])

    def attend_window(n, carry):
        w = lax.rem(3 * n, 4)
        for g in range(4):
            attend(w, g)
        mixed = attended_t[:, :, :, pl.ds(pl.multiple_of(w * 128, 128), 128)].reshape(512, 128).T
        branch[w] = dot(mixed, w_proj[...]).astype(bf16).reshape(2, 64, 512)
        second.begin_rows(w)
        return carry

    loads[1].wait()
    lax.fori_loop(0, 2, attend_window, 0)
    second.begin_rim((0, 3))
    lax.fori_loop(2, 4, attend_window, 0)
    pairs.append(send(attended_t.at[:, 1 - core], sib_attended, asem.at[1], arsem.at[1], where["sibling"]))
    second.arrive()
    for level in range(2):
        back = second.gather(level, to_patch).reshape(4, 64, 512)
        hidden[:, level] = (x_patch[:, level].astype(f32) + back.astype(bf16).astype(f32)).astype(bf16)

    def patches(ref):
        return jnp.concatenate([ref[q].reshape(128, 512) for q in range(4)], axis=1)

    gain_merge = gain_merge_ref[...]
    cells = patches(hidden).astype(f32)
    average = jnp.mean(cells, axis=-1, keepdims=True)
    centred = cells - average
    rstd = lax.rsqrt(jnp.mean(centred * centred, axis=-1, keepdims=True) + epsilon)
    hat = centred * rstd
    hat_m[...] = hat
    rstd_m[...] = jnp.broadcast_to(rstd, (128, 128))
    scaled = (hat * gain_merge).astype(bf16)
    for q in range(4):
        merged[q] = scaled[:, q * 512 : (q + 1) * 512]

    def part_rows(target, y, value):
        value = value.T.reshape(2, 4, 2, 16, 128)
        for c in range(2):
            for z in range(2):
                target[c, z, y] = value[c, :, z]

    for q in range(4):
        turned = scaled[:, q * 512 : (q + 1) * 512].T.reshape(2, 256, 128)
        for c in range(2):
            merged_t[c, q] = turned[c]
    side, level_z = 1 - core, where["z"]
    merged_side = share(3, merged_t.at[side], mergeds, "sibling")

    loads[2].wait()
    bend = 0.7978845608028654

    def merge(n, carry):
        rows = jnp.concatenate([merged[q] for q in range(4)], axis=1)
        coarse = dot(rows, w_merge[:, pl.ds(pl.multiple_of(n * 256, 256), 256)])
        square = coarse * coarse
        bent = jnp.tanh(bend * (coarse + 0.044715 * (coarse * square)))
        active = (0.5 * coarse * (1.0 + bent)).astype(bf16)
        act[n] = active
        part_rows(act_t, n, active)
        inner = bend * (1.0 + 3.0 * 0.044715 * square)
        slope[n] = 0.5 * (1.0 + bent) + 0.5 * coarse * (1.0 - bent * bent) * inner
        return carry

    lax.fori_loop(0, 4, merge, 0)
    act_parts = [
        share(6, act_t.at[side, level_z], acts.at[0], "sibling"),
        share(7, act_t.at[core, 1 - level_z], acts.at[1], "beside"),
        share(8, act_t.at[side, 1 - level_z], acts.at[2], "corner"),
    ]

    loads[3].wait()

    def back_expand(n, carry):
        rows = patches(c_patch)
        slab = w_expand[pl.ds(pl.multiple_of(n * 256, 256), 256), :]
        gcoarse[n] = (slope[n] * dot_nt(rows, slab)).astype(bf16)
        return carry

    lax.fori_loop(0, 4, back_expand, 0)
    gcoarse_side = share(9, gcoarse, gcoarses, "sibling")
    cot_beside.wait_recv()
    cot_corner = share(2, cots.at[1], cots.at[2], "sibling")

    def store_q1(value):
        qkv_out[:, 0:768] = value

    def store_q2(value):
        qkv_out[:, 768:1536] = value

    def store_pj(value):
        proj_out[...] = value

    def store_ex(value):
        ex_out[...] = value

    def store_mg(value):
        mg_out[:, 0:768] = value

    def store_mh(value):
        mg_out[:, 768:1024] = value

    stream_ex = Stream(where, acc_ex, "y", False, streams_scratch[0], store_ex)
    stream_mg = Stream(where, acc_mg, "x", True, streams_scratch[1], store_mg)
    stream_pj = Stream(where, acc_pj, "x", True, streams_scratch[2], store_pj)
    stream_q1 = Stream(where, acc_q1, "y", True, streams_scratch[3], store_q1)
    stream_q2 = Stream(where, acc_q2, "x", True, streams_scratch[4], store_q2)
    stream_mh = Stream(where, acc_mh, "y", True, streams_scratch[5], store_mh)
    def back_merge(q, carry):
        rows = jnp.concatenate([gcoarse[n] for n in range(4)], axis=1)
        slab = w_merge[pl.ds(pl.multiple_of(q * 512, 512), 512), :]
        ghidden[q] = dot_nt(rows, slab).reshape(2, 64, 512)
        return carry

    lax.fori_loop(0, 4, back_merge, 0)
    gain = [gain_merge[:, q * 512 : (q + 1) * 512] for q in range(4)]
    first_sum = jnp.zeros((128, 1), f32)
    second_sum = jnp.zeros((128, 1), f32)
    for q in range(4):
        grad = ghidden[q].reshape(128, 512) * gain[q]
        first_sum += jnp.sum(grad, axis=-1, keepdims=True)
        second_sum += jnp.sum(grad * hat_m[:, q * 512 : (q + 1) * 512], axis=-1, keepdims=True)
    first_sum, second_sum = first_sum / 2048.0, second_sum / 2048.0
    rstd = rstd_m[:, 0:1]
    for q in range(4):
        grad = ghidden[q].reshape(128, 512) * gain[q]
        grad = rstd * (grad - first_sum - hat_m[:, q * 512 : (q + 1) * 512] * second_sum)
        grad = grad + c_patch[q].reshape(128, 512).astype(f32)
        ghidden[q] = grad.reshape(2, 64, 512)
        gbranch[q] = grad.astype(bf16).reshape(2, 64, 512)

    third = Exchange(where, gbranch, pack_patch, exchanges[2])
    third.begin()

    merged_side.wait_recv()
    gcoarse_side.wait_recv()

    def merge_part(n):
        parts = [merged_t[core].reshape(1024, 128), mergeds[...].reshape(1024, 128)]
        left = jnp.concatenate(parts, axis=1)
        right = jnp.concatenate((gcoarse[n], gcoarses[n]), axis=0)
        return dot(left, right).astype(bf16).reshape(4, 4, 64, 256)

    def grad_merge(n, carry):
        acc_mg[:, :, :, pl.ds(pl.multiple_of(n * 256, 256), 256)] = merge_part(n)
        return carry

    lax.fori_loop(0, 3, grad_merge, 0)
    stream_mg.ring.begin()
    acc_mh[...] = merge_part(3)
    stream_mh.ring.begin()
    for made in act_parts:
        made.wait_recv()
    cot_side.wait_recv()
    cot_corner.wait_recv()

    def grad_expand(q, carry):
        parts = [act_t[core, level_z]] + [acts[n] for n in range(3)]
        left = jnp.concatenate([part.reshape(256, 128) for part in parts], axis=1)
        parts = [c_patch[q]] + [cots[n, q] for n in range(3)]
        right = jnp.concatenate([part.reshape(128, 512) for part in parts], axis=0)
        got = dot(left, right).astype(bf16).reshape(4, 4, 16, 512)
        acc_ex[:, :, :, pl.ds(pl.multiple_of(q * 512, 512), 512)] = got
        return carry

    lax.fori_loop(0, 4, grad_expand, 0)
    stream_ex.ring.begin()

    third.arrive()
    for level in range(2):
        gbranch_w[:, level] = third.gather(level, to_window).astype(bf16).reshape(4, 64, 512)
    grads_w = gbranch_w[...].reshape(512, 512)
    gattended[...] = dot_nt(grads_w, w_proj[...]).astype(bf16).reshape(4, 128, 512)
    turned = dot_nt(w_proj[...], grads_w).astype(bf16)
    for w in range(4):
        gattended_t[w] = turned[:, w * 128 : (w + 1) * 128].reshape(4, 128, 128)
    pairs.append(send(gbranch_w, sib_gbranch, asem.at[2], arsem.at[2], where["sibling"]))

    def share_window(w):
        return pltpu.make_async_remote_copy(
            src_ref=gqkv.at[:, w],
            dst_ref=sib_gqkv.at[:, w],
            send_sem=asem.at[3 + w],
            recv_sem=arsem.at[3 + w],
            device_id=where["sibling"],
            device_id_type=MESH,
        )

    def attend_back(w, g):
        grads = gattended[w, :, g * 128 : (g + 1) * 128]
        grad_weights = dot(qkv[8 + g, w], head_blocks(gattended_t[w, g]))
        weight = weights[w, g]
        wide = weight.astype(f32)
        shared = wide * grad_weights
        delta = jnp.sum(shared, axis=0, keepdims=True)
        grad_scores = ((shared - wide * delta) * scale).astype(bf16)
        turned = dot(head_blocks(qkv_t[4 + g, w]), under(grad_scores))
        gqkv[g, w] = turned.astype(bf16).T
        gqkv[4 + g, w] = dot(grad_scores, head_stack(qkv[g, w])).astype(bf16)
        gqkv[8 + g, w] = dot(weight, head_stack(grads)).astype(bf16)

    def attend_back_window(w, carry):
        for g in range(4):
            attend_back(w, g)
        share_window(w).start()
        return carry

    lax.fori_loop(0, 2, attend_back_window, 0)
    for made in pairs:
        made.wait_recv()
    left = jnp.concatenate((attended_t[:, core].reshape(256, 512), sib_attended[...].reshape(256, 512)), axis=1)
    right = jnp.concatenate((gbranch_w[...].reshape(512, 512), sib_gbranch[...].reshape(512, 512)), axis=0)
    acc_pj[...] = dot(left, right).astype(bf16).reshape(4, 4, 16, 512)
    stream_pj.ring.begin()
    stream_ex.ring.middle()
    stream_mg.ring.middle()
    stream_mh.ring.middle()
    lax.fori_loop(2, 4, attend_back_window, 0)
    windows = [share_window(w) for w in range(4)]
    for made in windows:
        made.wait_recv()

    def grad_qkv(target, base, n, carry):
        left = jnp.concatenate((normed_t[:, core].reshape(256, 512), sib_normed[...].reshape(256, 512)), axis=1)
        k = 2 * n + base
        own = [gqkv[k + part].reshape(512, 128) for part in range(2)]
        far = [sib_gqkv[k + part].reshape(512, 128) for part in range(2)]
        right = jnp.concatenate((jnp.concatenate(own, axis=1), jnp.concatenate(far, axis=1)), axis=0)
        got = dot(left, right).astype(bf16).reshape(4, 4, 16, 256)
        target[:, :, :, pl.ds(pl.multiple_of(n * 256, 256), 256)] = got
        return carry

    lax.fori_loop(0, 3, functools.partial(grad_qkv, acc_q1, 0), 0)
    stream_q1.ring.begin()
    lax.fori_loop(0, 3, functools.partial(grad_qkv, acc_q2, 6), 0)
    stream_q2.ring.begin()
    stream_mg.ring.finish()
    stream_mg.spread()
    stream_mh.ring.finish()
    stream_mh.spread()
    stream_ex.ring.finish()
    stream_ex.spread()

    def norm_back(half, carry):
        rows = jnp.concatenate([gqkv[n, pl.ds(2 * half, 2)].reshape(256, 128) for n in range(12)], axis=1)
        grad = dot_nt(rows, w_qkv[...]) * gain_attn
        hat = hat_w[pl.ds(2 * half, 2)].reshape(256, 512)
        rstd = rstd_w[pl.ds(2 * half, 2)].reshape(256, 128)[:, 0:1]
        first_mean = jnp.mean(grad, axis=-1, keepdims=True)
        second_mean = jnp.mean(grad * hat, axis=-1, keepdims=True)
        grad = rstd * (grad - first_mean - hat * second_mean)
        grolled[pl.ds(2 * half, 2)] = grad.astype(bf16).reshape(2, 2, 64, 512)
        return carry

    lax.fori_loop(0, 2, norm_back, 0)
    fourth = Exchange(where, grolled, pack_window, exchanges[3])
    fourth.begin()
    stream_pj.ring.middle()
    stream_q1.ring.middle()
    stream_q2.ring.middle()

    writes = []
    fine_hot = one_hot(fine_code(iota((256, 256), 0)) == patch_code(iota((1, 256), 1)))

    def expand(q, carry):
        rows = jnp.concatenate([act[n] for n in range(4)], axis=1)
        grown = dot(rows, w_expand[:, pl.ds(pl.multiple_of(q * 512, 512), 512)])
        out_patch[q] = (hidden[q].reshape(128, 512).astype(f32) + grown).astype(bf16).reshape(2, 64, 512)
        return carry

    lax.fori_loop(0, 4, expand, 0)
    for level in range(2):
        out_ref[level] = dot(fine_hot, out_patch[:, level].reshape(256, 512)).astype(bf16)
        writes.append(pltpu.make_async_copy(out_ref.at[level], out_hbm.at[level], wsem.at[5 + level]))
        writes[-1].start()

    stream_pj.ring.finish()
    stream_pj.spread()
    stream_q1.ring.finish()
    stream_q1.spread()
    stream_q2.ring.finish()
    stream_q2.spread()
    fourth.arrive()
    for level in range(2):
        back = fourth.gather(level, to_patch).astype(bf16).astype(f32)
        total = (ghidden[:, level].reshape(256, 512) + back).astype(bf16)
        field_ref[level] = dot(fine_hot, total).astype(bf16)
        writes.append(pltpu.make_async_copy(field_ref.at[level], field_hbm.at[level], wsem.at[7 + level]))
        writes[-1].start()

    streams = (stream_ex, stream_mh, stream_mg, stream_pj, stream_q1, stream_q2)
    for stream in streams:
        stream.end()

    for made in sent + pairs + windows:
        made.wait_send()
    for made in writes:
        made.wait()
    for each in (first, second, third, fourth):
        each.drain()
    for stream in streams:
        stream.drain()


def deliver_kernel(*refs):
    sources, targets, held, sems = refs[:6], refs[6:12], refs[12:18], refs[18]
    pieces = []
    for array in zip(sources, held, targets):
        if len(array[0].shape) == 3:
            for level in range(2):
                for part in range(2):
                    pieces.append([ref.at[level, pl.ds(part * 128, 128)] for ref in array])
        else:
            pieces.append(array)
    loads = [pltpu.make_async_copy(a, b, sems.at[0, n]) for n, (a, b, _c) in enumerate(pieces)]
    stores = [pltpu.make_async_copy(b, c, sems.at[1, n]) for n, (_a, b, c) in enumerate(pieces)]
    for made in loads:
        made.start()
    for load, store in zip(loads, stores):
        load.wait()
        store.start()
    for made in stores:
        made.wait()


def deliver(results):
    hbm = pl.BlockSpec(memory_space=pl.ANY)
    return pl.pallas_call(
        deliver_kernel,
        out_shape=tuple(jax.ShapeDtypeStruct(r.shape, r.dtype) for r in results),
        in_specs=[hbm] * 6,
        out_specs=(hbm,) * 6,
        scratch_shapes=[pltpu.VMEM(r.shape, r.dtype) for r in results] + [pltpu.SemaphoreType.DMA((2, 12))],
        name="deliver",
    )(*results)


def on_device(
    fine_field,
    cotangent,
    land_sea,
    shifts,
    gain_attn,
    w_qkv,
    w_proj,
    land_bias,
    gain_merge,
    w_merge,
    w_expand,
):
    vmem = pl.BlockSpec(memory_space=pltpu.VMEM)
    smem = pl.BlockSpec(memory_space=pltpu.SMEM)
    hbm = pl.BlockSpec(memory_space=pl.ANY)
    f32, bf16 = jnp.float32, jnp.bfloat16
    cells = (4, 2, 64, 512)
    scratch = [
        pltpu.VMEM((512, 1536), bf16),
        pltpu.VMEM((512, 512), bf16),
        pltpu.VMEM((2048, 1024), bf16),
        pltpu.VMEM((1024, 2048), bf16),
        pltpu.VMEM((2, 256, 512), bf16),
        pltpu.VMEM((2, 256, 512), bf16),
        pltpu.VMEM((2, 256, 512), bf16),
        pltpu.SemaphoreType.DMA((9,)),
        pltpu.VMEM((256, 640), bf16),
        pltpu.VMEM((256, 640), bf16),
        pltpu.VMEM((64, 256), bf16),
        pltpu.VMEM((64, 256), bf16),
        pltpu.VMEM(cells, bf16),
        pltpu.VMEM(cells, bf16),
        pltpu.VMEM(cells, bf16),
        pltpu.VMEM(cells, f32),
        pltpu.VMEM((4, 2, 64, 128), f32),
        pltpu.VMEM((12, 4, 128, 128), bf16),
        pltpu.VMEM((12, 4, 128, 128), bf16),
        pltpu.VMEM((4, 4, 128, 512), bf16),
        pltpu.VMEM(cells, bf16),
        pltpu.VMEM(cells, bf16),
        pltpu.VMEM((128, 2048), f32),
        pltpu.VMEM((128, 128), f32),
        pltpu.VMEM((4, 128, 512), bf16),
        pltpu.VMEM((4, 128, 256), f32),
        pltpu.VMEM((4, 128, 256), bf16),
        pltpu.VMEM((4, 128, 256), bf16),
        pltpu.VMEM(cells, bf16),
        pltpu.VMEM(cells, f32),
        pltpu.VMEM(cells, bf16),
        pltpu.VMEM((3,) + cells, bf16),
        pltpu.VMEM((4, 128, 256), bf16),
        pltpu.VMEM((2, 2, 4, 4, 16, 128), bf16),
        pltpu.VMEM((2, 4, 256, 128), bf16),
        pltpu.VMEM((3, 4, 4, 16, 128), bf16),
        pltpu.VMEM((4, 256, 128), bf16),
        pltpu.SemaphoreType.DMA((12,)),
        pltpu.SemaphoreType.DMA((12,)),
        pltpu.VMEM(cells, bf16),
        pltpu.VMEM((4, 128, 512), bf16),
        pltpu.VMEM((4, 4, 128, 128), bf16),
        pltpu.VMEM((12, 4, 128, 128), bf16),
        pltpu.VMEM(cells, bf16),
        pltpu.VMEM(cells, bf16),
        pltpu.VMEM(cells, bf16),
        pltpu.VMEM((4, 64, 512), bf16),
        pltpu.VMEM((4, 64, 512), bf16),
        pltpu.VMEM(cells, bf16),
        pltpu.VMEM((12, 4, 128, 128), bf16),
        pltpu.SemaphoreType.DMA((7,)),
        pltpu.SemaphoreType.DMA((7,)),
        pltpu.VMEM((4, 4, 16, 2048), bf16),
        pltpu.VMEM((4, 4, 64, 768), bf16),
        pltpu.VMEM((4, 4, 64, 256), bf16),
        pltpu.VMEM((4, 4, 16, 512), bf16),
        pltpu.VMEM((4, 4, 16, 768), bf16),
        pltpu.VMEM((4, 4, 16, 768), bf16),
    ]
    for _ in range(4):
        scratch += exchange_scratch()
    scratch += stream_scratch(16, 2048, False)
    scratch += stream_scratch(64, 768, True)
    scratch += stream_scratch(16, 512, True)
    scratch += stream_scratch(16, 768, True)
    scratch += stream_scratch(16, 768, True)
    scratch += stream_scratch(64, 256, True)
    scratch += [pltpu.VMEM((4, 128, 128), f32)]
    results = pl.pallas_call(
        block_kernel,
        out_shape=(
            jax.ShapeDtypeStruct((2, 256, 512), bf16),
            jax.ShapeDtypeStruct((2, 256, 512), bf16),
            jax.ShapeDtypeStruct((8, 1536), f32),
            jax.ShapeDtypeStruct((8, 512), f32),
            jax.ShapeDtypeStruct((32, 1024), f32),
            jax.ShapeDtypeStruct((16, 2048), f32),
        ),
        in_specs=[smem, smem, vmem, hbm] + [vmem] * 3 + [hbm] * 4,
        out_specs=(hbm, hbm) + (vmem,) * 4,
        scratch_shapes=scratch,
        compiler_params=pltpu.CompilerParams(
            collective_id=0, has_side_effects=True, vmem_limit_bytes=60 * 2**20
        ),
        name="attention_block",
    )(
        shifts,
        land_bias,
        fine_field.reshape(2, 256, 512),
        cotangent.reshape(2, 256, 512),
        land_sea,
        gain_attn.reshape(1, 512),
        gain_merge.reshape(1, 2048),
        w_qkv,
        w_proj,
        w_merge,
        w_expand,
    )
    results = deliver(results)
    output, grad_field = results[0].reshape(2, 8, 32, 512), results[1].reshape(2, 8, 32, 512)
    return (output, grad_field) + tuple(results[2:])


def solution(mesh):
    return jax.shard_map(
        on_device,
        mesh=mesh,
        in_specs=(
            P("rep", "lat", "lon", None),
            P("rep", "lat", "lon", None),
            P(),
            P(),
            P(),
            P(),
            P(),
            P(),
            P(),
            P(),
            P(),
        ),
        out_specs=(
            P("rep", "lat", "lon", None),
            P("rep", "lat", "lon", None),
            P(("rep", "lat", "lon"), None),
            P(("rep", "lat", "lon"), None),
            P(("rep", "lat", "lon"), None),
            P(("rep", "lat", "lon"), None),
        ),
        check_vma=False,
    )
```
